256 devices in a mesh: gx: 8 (over x, z_lo), gy: 4 (over y), gz: 8 (over z_hi, core).
Axes of the slice: x: 4, y: 4, z: 8 (z_hi: 4, z_lo: 2; z = z_hi * 2 + z_lo), core: 2. Of those that a mesh axis runs over, the one named last changes fastest.
Arguments:
- tokens: bfloat16 [65536, 768], P(('gx', 'gy', 'gz')), may hold values from -6 to 6
- norm_gain: float32 [768], replicated, may hold values from 0.5 to 1.5
- w_qkv: bfloat16 [768, 2304], replicated
- w_out: bfloat16 [768, 768], replicated, may hold values from -0.21875 to 0.21875
- send_rows: int32 [256, 7, 32], P(('gx', 'gy', 'gz')), may hold values from -1 to 255, as said below
- window_rows: int32 [256, 512], P(('gx', 'gy', 'gz')), may hold values from -1 to 479, as said below
- grad_out: bfloat16 [65536, 768], P(('gx', 'gy', 'gz')), may hold values from -6 to 6
Outputs:
- block_out: bfloat16 [65536, 768], P(('gx', 'gy', 'gz'))
- grad_tokens: bfloat16 [65536, 768], P(('gx', 'gy', 'gz'))
- grad_gain: float32 [768], P(('gx', 'gy', 'gz'))
- grad_w_qkv: float32 [768, 2304], P(('gx', 'gy', 'gz'))
- grad_w_out: float32 [768, 768], P(('gx', 'gy', 'gz'))
The draws below stay inside these ranges and needn't reach their ends.
Inputs may be any that keep to these rules, and one draw needn't show every extreme that they name: `send_rows`: entries are rows of the tile (0 to 255) or -1 for empty; in each list the rows come first; a row stands in at most one list of its tile; a tile at the upper end of an axis has no rows in lists toward that axis; tile 0 fills all 7 lists. `window_rows`: entries index the owner's row list (256 own rows, then the 7 received lists of 32 in order k) or are -1 for padding; every own row that no list sends away and every non-empty received entry fills exactly one slot, nothing else does; a device's filled slots make whole windows but one.
All inputs are finite; a program needn't handle non-finite values.
Results may differ from the reference program's by a relative error of at most 0.018.
Values may be sent and summed in bfloat16 or wider, within the bound.
No kernel may reach another device: no remote copies, remote signals or barrier semaphores. Data moves between devices by JAX's collectives and lax.ppermute only.
A program may use at most 128 MiB of HBM per device.

```python
import math
import jax
import jax.numpy as jnp
from jax import lax

D = 768
HEADS = 12
HDIM = 64
TOK_DEV = 256
WCAP = 128
WIN_DEV = 4
SLOTS = 512
TOKENS = 65536
N_GX = 8
N_GY = 4
N_GZ = 8


def layout(key):
    devices = N_GX * N_GY * N_GZ
    bcap = TOK_DEV // 8
    span = TOK_DEV + 7 * bcap
    slots = WIN_DEV * WCAP
    key_order, key_count, key_fill, key_window = jax.random.split(key, 4)
    orders = jax.vmap(lambda k: jax.random.permutation(k, TOK_DEV))(jax.random.split(key_order, devices)).astype(jnp.int32)
    orders = (orders + (TOK_DEV - 1) - orders[:, :1]) % TOK_DEV
    counts = jax.random.randint(key_count, (devices, 7), max(bcap // 2, 1), bcap + 1).astype(jnp.int32)
    device = jnp.arange(devices, dtype=jnp.int32)
    coord_x = device // (N_GY * N_GZ)
    coord_y = device // N_GZ % N_GY
    coord_z = device % N_GZ
    direction = jnp.arange(1, 8, dtype=jnp.int32)
    step_x = direction // 4
    step_y = direction // 2 % 2
    step_z = direction % 2
    leaves = (coord_x[:, None] + step_x[None, :] >= N_GX) | (coord_y[:, None] + step_y[None, :] >= N_GY) | (coord_z[:, None] + step_z[None, :] >= N_GZ)
    counts = jnp.where(leaves, 0, counts)
    counts = counts.at[0].set(bcap)
    position = jnp.arange(bcap, dtype=jnp.int32)
    base = (direction[:, None] - 1) * bcap + position[None, :]
    chosen = orders[:, base]
    send = jnp.where(position[None, None, :] < counts[:, :, None], chosen, -1).astype(jnp.int32)
    ranks = jax.vmap(lambda o: jnp.zeros(TOK_DEV, jnp.int32).at[o].set(jnp.arange(TOK_DEV, dtype=jnp.int32)))(orders)
    block = jnp.minimum(ranks // bcap, 6)
    limit = jnp.take_along_axis(counts, block, axis=1)
    kept = (ranks >= 7 * bcap) | (ranks % bcap >= limit)
    src_x = coord_x[:, None] - step_x[None, :]
    src_y = coord_y[:, None] - step_y[None, :]
    src_z = coord_z[:, None] - step_z[None, :]
    inside = (src_x >= 0) & (src_y >= 0) & (src_z >= 0)
    source = jnp.where(inside, (src_x * N_GY + src_y) * N_GZ + src_z, 0).astype(jnp.int32)
    entries = send[source, direction[None, :] - 1]
    arrived = inside[:, :, None] & (entries >= 0)
    valid = jnp.concatenate([kept, arrived.reshape(devices, 7 * bcap)], axis=1)
    scores = jax.vmap(lambda k: jax.random.permutation(k, span))(jax.random.split(key_fill, devices)).astype(jnp.int32)
    scores = jnp.where(valid, scores, scores + span)
    ordered = jnp.argsort(scores, axis=1, stable=True).astype(jnp.int32)
    filled = jnp.sum(valid.astype(jnp.int32), axis=1)
    place = jnp.arange(slots, dtype=jnp.int32)
    sequence = jnp.where(place[None, :] < filled[:, None], ordered[:, jnp.minimum(place, span - 1)], -1)
    key_outer, key_inner = jax.random.split(key_window, 2)
    window_order = jax.vmap(lambda k: jax.random.permutation(k, WIN_DEV))(jax.random.split(key_outer, devices)).astype(jnp.int32)
    inner_order = jax.vmap(lambda k: jax.random.permutation(k, WCAP))(jax.random.split(key_inner, devices * WIN_DEV)).astype(jnp.int32)
    inner_order = inner_order.reshape(devices, WIN_DEV, WCAP)
    index = (window_order[:, :, None] * WCAP + inner_order).reshape(devices, slots)
    table = jnp.take_along_axis(sequence, index, axis=1).astype(jnp.int32)
    return (send, table)


def draw_send_rows(key, part):
    shared = layout(key)
    return shared[0]


def draw_window_rows(key, part):
    shared = layout(key)
    return shared[1]


def draw_w_qkv(key, part):
    key = jax.random.fold_in(key, 3)
    base = jnp.clip(jax.random.normal(key, (D, 3 * D), jnp.float32), -4.0, 4.0) / math.sqrt(D)
    return base.astype(jnp.bfloat16)


def levels(key, extent, pieces, least, high):
    gain = 1.0
    for dim, blocks in pieces:
        steps = jax.random.uniform(jax.random.fold_in(jax.random.fold_in(key, 6), dim), (blocks,), jnp.float32, least / len(pieces), high / len(pieces))
        gain = gain * jnp.repeat(jnp.exp(steps), extent[dim] // blocks).reshape((-1,) + (1,) * (len(extent) - 1 - dim))
    return gain


def bell_draw(own_key, shape, scale, most, shards=(), held_as=jnp.bfloat16):
    level = levels(own_key, shape, shards, -0.22, 0.18) if shards else 1.0
    drawn = jax.random.normal(own_key, shape, jnp.float32) * scale * level
    return jnp.minimum(jnp.maximum(drawn, -most), most).astype(held_as)


def setup_inputs(seed: int = 0) -> dict:
    splits = jax.random.split(jax.random.key(seed), 8)
    tokens = bell_draw(splits[0], (TOKENS, D), 1.0, 6.0, ((0, 256),))
    norm_gain = jnp.clip(1.0 + 0.1 * jax.random.normal(splits[1], (D,), jnp.float32), 0.5, 1.5)
    w_qkv = draw_w_qkv(jax.random.fold_in(splits[7], 71), 0)
    w_out = bell_draw(splits[3], (D, D), D ** -0.5, 0.21875)
    send_rows = draw_send_rows(jax.random.fold_in(splits[7], 71), 0)
    window_rows = draw_window_rows(jax.random.fold_in(splits[7], 71), 0)
    grad_out = bell_draw(splits[6], (TOKENS, D), 1.0, 6.0, ((0, 256),))
    return {"tokens": tokens, "norm_gain": norm_gain, "w_qkv": w_qkv, "w_out": w_out, "send_rows": send_rows, "window_rows": window_rows, "grad_out": grad_out}


epsilon = 1e-06
big_negative = -1e+30

def take_rows(table, index):
    safe = jnp.maximum(index, 0).astype(jnp.int32)
    taken = jnp.take(table, safe, axis=0)
    return jnp.where((index >= 0)[..., None], taken, jnp.zeros((), table.dtype))

def spread_rows(values, index, length):
    target = jnp.where(index >= 0, index, length).astype(jnp.int32)
    empty = jnp.zeros((length, values.shape[-1]), values.dtype)
    return empty.at[target].set(values, mode='drop')

def slot_tokens(send_rows, window_rows):
    devices = N_GX * N_GY * N_GZ
    device = jnp.arange(devices, dtype=jnp.int32)
    coord_x = device // (N_GY * N_GZ)
    coord_y = device // N_GZ % N_GY
    coord_z = device % N_GZ
    columns = [device[:, None] * TOK_DEV + jnp.arange(TOK_DEV, dtype=jnp.int32)[None, :]]
    for direction in range(1, 8):
        src_x = coord_x - direction // 4
        src_y = coord_y - direction // 2 % 2
        src_z = coord_z - direction % 2
        inside = (src_x >= 0) & (src_y >= 0) & (src_z >= 0)
        source = jnp.where(inside, (src_x * N_GY + src_y) * N_GZ + src_z, 0).astype(jnp.int32)
        entries = send_rows[source, direction - 1]
        usable = inside[:, None] & (entries >= 0)
        columns.append(jnp.where(usable, source[:, None] * TOK_DEV + entries, -1).astype(jnp.int32))
    table = jnp.concatenate(columns, axis=1)
    picked = jnp.take_along_axis(table, jnp.maximum(window_rows, 0).astype(jnp.int32), axis=1)
    return jnp.where(window_rows >= 0, picked, -1).astype(jnp.int32)

def split_heads(packed):
    split = packed.reshape(WIN_DEV, WCAP, 3, HEADS, HDIM).astype(jnp.float32)
    return (split[:, :, 0], split[:, :, 1], split[:, :, 2])

def attend(packed, valid):
    query, keys, values = split_heads(packed)
    scores = jnp.einsum('wqhd,wkhd->whqk', query, keys) * HDIM ** (-0.5)
    scores = jnp.where(valid[:, None, None, :], scores, big_negative)
    top = lax.optimization_barrier(jnp.max(scores, axis=-1, keepdims=True))
    expo = jnp.exp(scores - top)
    probs = expo / lax.optimization_barrier(jnp.sum(expo, axis=-1, keepdims=True))
    weights = lax.optimization_barrier(probs.astype(jnp.bfloat16))
    mixed = jnp.einsum('whqk,wkhd->wqhd', weights.astype(jnp.float32), values).astype(jnp.bfloat16)
    return (mixed.reshape(SLOTS, D), probs, weights)

def attend_back(packed, probs, weights, delta_slots):
    query, keys, values = split_heads(packed)
    grad_delta = delta_slots.reshape(WIN_DEV, WCAP, HEADS, HDIM).astype(jnp.float32)
    dweights = jnp.einsum('wqhd,wkhd->whqk', grad_delta, values)
    dscores = probs * (dweights - lax.optimization_barrier(jnp.sum(dweights * probs, axis=-1, keepdims=True)))
    dscaled = lax.optimization_barrier((dscores * HDIM ** (-0.5)).astype(jnp.bfloat16)).astype(jnp.float32)
    dquery = jnp.einsum('whqk,wkhd->wqhd', dscaled, keys)
    dkeys = jnp.einsum('whqk,wqhd->wkhd', dscaled, query)
    dvalues = jnp.einsum('whqk,wqhd->wkhd', weights.astype(jnp.float32), grad_delta)
    joined = jnp.stack([dquery, dkeys, dvalues], axis=2)
    return joined.reshape(SLOTS, 3 * D).astype(jnp.bfloat16)

def reference(tokens, norm_gain, w_qkv, w_out, send_rows, window_rows, grad_out):
    floats = tokens.astype(jnp.float32)
    centred = floats - lax.optimization_barrier(jnp.mean(floats, axis=-1, keepdims=True))
    inv_std = lax.rsqrt(lax.optimization_barrier(jnp.mean(centred * centred, axis=-1, keepdims=True)) + epsilon)
    unit = centred * inv_std
    normed = (unit * norm_gain).astype(jnp.bfloat16)
    packed_all = jnp.dot(normed, w_qkv, preferred_element_type=jnp.float32).astype(jnp.bfloat16)
    slot_ids = slot_tokens(send_rows, window_rows)

    def forward_one(index):
        packed = take_rows(packed_all, index)
        mixed, probs, weights = attend(packed, (index >= 0).reshape(WIN_DEV, WCAP))
        return mixed
    mixed_all = lax.map(forward_one, slot_ids)
    attended = spread_rows(mixed_all.reshape(-1, D), slot_ids.reshape(-1), TOKENS)
    block_out = (floats + jnp.dot(attended, w_out, preferred_element_type=jnp.float32)).astype(jnp.bfloat16)
    grad_w_out = jnp.dot(attended.T, grad_out, preferred_element_type=jnp.float32)
    delta = jnp.dot(grad_out, w_out.T, preferred_element_type=jnp.float32).astype(jnp.bfloat16)

    def backward_one(index):
        packed = take_rows(packed_all, index)
        mixed, probs, weights = attend(packed, (index >= 0).reshape(WIN_DEV, WCAP))
        return attend_back(packed, probs, weights, take_rows(delta, index))
    dpacked_slots = lax.map(backward_one, slot_ids)
    dpacked = spread_rows(dpacked_slots.reshape(-1, 3 * D), slot_ids.reshape(-1), TOKENS)
    grad_w_qkv = jnp.dot(normed.T, dpacked, preferred_element_type=jnp.float32)
    dnormed = jnp.dot(dpacked, w_qkv.T, preferred_element_type=jnp.float32).astype(jnp.bfloat16)
    dnormed_f = dnormed.astype(jnp.float32)
    grad_gain = lax.optimization_barrier(jnp.sum(dnormed_f * unit, axis=0))
    dunit = dnormed_f * norm_gain
    dcentre = inv_std * (dunit - lax.optimization_barrier(jnp.mean(dunit, axis=-1, keepdims=True)) - unit * lax.optimization_barrier(jnp.mean(dunit * unit, axis=-1, keepdims=True)))
    grad_tokens = (grad_out.astype(jnp.float32) + dcentre).astype(jnp.bfloat16)
    return (block_out, grad_tokens, grad_gain, grad_w_qkv, grad_w_out)
```

```python
import functools
import itertools

import jax
import jax.numpy as jnp
from jax import lax
from jax.experimental import pallas as pl
from jax.experimental.pallas import tpu as pltpu
from jax.sharding import PartitionSpec as P

D = 768
WCAP = 128
SLOTS = 512
ROWS = 256
WIDE = 2 * D
COLS_A = 2 * D
COLS_B = 2 * D + 128
COLS = COLS_A + COLS_B
AXES = ("gx", "gy", "gz")
EPSILON = 1e-06
BIG_NEGATIVE = -1e30
BF = jnp.bfloat16
F32 = jnp.float32
NT = (((1,), (1,)), ((), ()))
TN = (((0,), (0,)), ((), ()))
PARAMS = pltpu.CompilerParams(vmem_limit_bytes=56 * 1024 * 1024)
VMEM = pl.BlockSpec(memory_space=pltpu.VMEM)


def dot(a, b):
    return jnp.dot(a, b, preferred_element_type=F32)


def iota(shape, dim):
    return lax.broadcasted_iota(jnp.int32, shape, dim)


def column(row):
    n = row.shape[1]
    spread = jnp.broadcast_to(row.astype(F32), (n, n))
    return jnp.sum(jnp.where(iota((n, n), 0) == iota((n, n), 1), spread, 0.0), axis=1, keepdims=True)


def one_hot(condition):
    return jnp.where(condition, 1.0, 0.0).astype(BF)


def passed_along(value, axis, steps):
    count = lax.axis_size(axis)
    initial, last = (max(0, -steps), min(count, count - steps))
    return lax.ppermute(value, axis, [(source, source + steps) for source in range(initial, last)])


def crossed(value, axis, mask):
    count = lax.axis_size(axis)
    return lax.ppermute(value, axis, [(source, source ^ mask) for source in range(count)])


def pack_body(tok_ref, go_ref, send_ref, out_ref):
    chosen = [
        one_hot(iota((32, ROWS), 1).astype(F32) == column(send_ref[0, k : k + 1, :])) for k in range(7)
    ]
    chosen = jnp.concatenate(chosen, axis=0)
    for part, ref in enumerate((tok_ref, go_ref)):
        taken = dot(chosen, ref[...]).astype(BF)
        out_ref[:, :, part * D : (part + 1) * D] = taken.reshape(7, 32, D)


def normalised(x):
    centred = x - jnp.mean(x, axis=-1, keepdims=True)
    inv_std = lax.rsqrt(jnp.mean(centred * centred, axis=-1, keepdims=True) + EPSILON)
    return centred * inv_std, inv_std


def order(me_ref, piece):
    j = iota((D, 1), 0)
    core = j // 384
    rest = j % 384
    if piece == 0:
        gx, gy = rest // 48, rest % 48 // 12
    else:
        gy, gx = rest // 96, rest % 96 // 12
    z_hi, r = rest % 12 // 3, rest % 3
    gx = gx ^ me_ref[0]
    gy = gy ^ me_ref[1]
    gz = (z_hi * 2 + core) ^ me_ref[2]
    return ((gx * 4 + gy) * 8 + gz) * 3 + r


def main_body(
    me_ref, tok_ref, go_ref, fx_ref, fy_ref, fz_ref, win_ref, gain_ref, wqkv_ref, wout_ref,
    own_ref, snd_ref, xs_ref, gos_ref, mixed_ref, dn_ref,
    rows_ref, normed_ref, unit_ref, packed_ref, delta_ref, dpacked_ref,
):
    rows_ref[:ROWS, :D] = tok_ref[...]
    rows_ref[:ROWS, D:] = go_ref[...]
    arrived = (
        fz_ref[0], fy_ref[0], fz_ref[1], fx_ref[0], fz_ref[2], fy_ref[2], fz_ref[3],
    )
    for k, block in enumerate(arrived):
        rows_ref[ROWS + 32 * k : ROWS + 32 * (k + 1), :] = block
    rows_ref[480:, :] = jnp.zeros((32, WIDE), BF)
    gain = gain_ref[...]

    def gather_window(w, carry):
        at = pl.ds(pl.multiple_of(w * WCAP, WCAP), WCAP)
        picks = one_hot(iota((WCAP, SLOTS), 1).astype(F32) == column(win_ref[:, at]))
        taken = dot(picks, rows_ref[...])
        x = taken[:, :D]
        xs_ref[at, :] = x.astype(BF)
        gos_ref[at, :] = taken[:, D:].astype(BF)
        unit, _ = normalised(x)
        unit_ref[at, :] = unit
        normed_ref[at, :] = (unit * gain).astype(BF)
        return carry

    lax.fori_loop(0, SLOTS // WCAP, gather_window, 0)

    def project(c, carry):
        at = pl.ds(pl.multiple_of(c * D, D), D)
        packed_ref[:, at] = dot(normed_ref[...], wqkv_ref[:, at]).astype(BF)
        return carry

    lax.fori_loop(0, 3, project, 0)
    delta_ref[...] = lax.dot_general(
        gos_ref[...], wout_ref[...], NT, preferred_element_type=F32
    ).astype(BF)

    low = iota((WCAP, 128), 1) < 64
    zero = jnp.zeros((), BF)

    def both(value):
        return jnp.concatenate([jnp.where(low, value, zero), jnp.where(low, zero, value)], axis=0)

    def attend(w, carry):
        at = pl.ds(pl.multiple_of(w * WCAP, WCAP), WCAP)
        filled = jnp.broadcast_to(column(win_ref[:, at]) >= 0, (WCAP, WCAP))[None]
        for p in range(6):
            q_at = pl.ds(p * 128, 128)
            k_at = pl.ds(D + p * 128, 128)
            v_at = pl.ds(2 * D + p * 128, 128)
            q = packed_ref[at, q_at]
            k_both = both(packed_ref[at, k_at])
            v_both = both(packed_ref[at, v_at])
            d = delta_ref[at, q_at]
            scores = lax.dot_general(k_both, q, NT, preferred_element_type=F32) * 0.125
            scores = jnp.where(filled, scores.reshape(2, WCAP, WCAP), BIG_NEGATIVE)
            expo = jnp.exp(scores - jnp.max(scores, axis=1, keepdims=True))
            probs = expo * (1.0 / jnp.sum(expo, axis=1, keepdims=True))
            weights = probs.astype(BF)
            mixed = lax.dot_general(
                weights.reshape(2 * WCAP, WCAP), v_both, TN, preferred_element_type=F32
            )
            mixed_ref[at, q_at] = mixed.astype(BF)
            dweights = lax.dot_general(v_both, d, NT, preferred_element_type=F32)
            dweights = dweights.reshape(2, WCAP, WCAP)
            inner = jnp.sum(dweights * probs, axis=1, keepdims=True)
            dscaled = (probs * (dweights - inner) * 0.125).astype(BF)
            dq = lax.dot_general(
                dscaled.reshape(2 * WCAP, WCAP), k_both, TN, preferred_element_type=F32
            )
            dpacked_ref[at, q_at] = dq.astype(BF)
            beside = jnp.concatenate([dscaled[0], dscaled[1]], axis=1)
            dpacked_ref[at, k_at] = dot(beside, both(q)).astype(BF)
            beside = jnp.concatenate([weights[0], weights[1]], axis=1)
            dpacked_ref[at, v_at] = dot(beside, both(d)).astype(BF)
        return carry

    lax.fori_loop(0, SLOTS // WCAP, attend, 0)

    dn = lax.dot_general(
        dpacked_ref[...], wqkv_ref[...], NT, preferred_element_type=F32
    ).astype(BF)
    dn_ref[...] = dn
    gain_row = jnp.sum(dn.astype(F32) * unit_ref[...], axis=0, keepdims=True)

    def halves(value, start):
        own_ref[:, pl.ds(start, value.shape[1])] = value[:384].astype(BF)
        snd_ref[:, pl.ds(start, value.shape[1])] = value[384:].astype(BF)

    place = iota((D, D), 1) == order(me_ref, 0)
    turned = lax.dot_general(
        one_hot(place), normed_ref[...], NT, preferred_element_type=F32
    ).astype(BF)
    for c in range(2):
        halves(dot(turned, dpacked_ref[:, c * D : (c + 1) * D]), c * D)
    place = iota((D, D), 1) == order(me_ref, 1)
    hot = one_hot(place)
    turned = lax.dot_general(hot, normed_ref[...], NT, preferred_element_type=F32).astype(BF)
    halves(dot(turned, dpacked_ref[:, 2 * D :]), 2 * D)
    turned = lax.dot_general(hot, mixed_ref[...], NT, preferred_element_type=F32).astype(BF)
    halves(dot(turned, gos_ref[...]), 3 * D)
    gain_col = jnp.sum(jnp.where(place, gain_row, 0.0), axis=1, keepdims=True)
    halves(jnp.broadcast_to(gain_col, (D, 128)), 4 * D)


def back_body(xs_ref, gos_ref, mixed_ref, dn_ref, win_ref, gain_ref, wout_ref, own_ref, ret_ref, cat_ref):
    gain = gain_ref[...]
    projected = dot(mixed_ref[...], wout_ref[...])
    cat_ref[:, :D] = (xs_ref[...].astype(F32) + projected).astype(BF)
    for w in range(4):
        at = slice(w * WCAP, (w + 1) * WCAP)
        unit, inv_std = normalised(xs_ref[at, :].astype(F32))
        dunit = dn_ref[at, :].astype(F32) * gain
        dcentre = inv_std * (
            dunit
            - jnp.mean(dunit, axis=-1, keepdims=True)
            - unit * jnp.mean(dunit * unit, axis=-1, keepdims=True)
        )
        cat_ref[at, D:] = (gos_ref[at, :].astype(F32) + dcentre).astype(BF)
    back = one_hot(iota((480, SLOTS), 0) == win_ref[...])
    own_ref[...] = dot(back[:ROWS], cat_ref[...]).astype(BF)
    ret_ref[...] = dot(back[ROWS:], cat_ref[...]).astype(BF).reshape(7, 32, WIDE)


def join_body(own_ref, dx_ref, dy_ref, dz_ref, send_ref, out_ref, grad_ref):
    arrived = (
        dz_ref[0], dy_ref[0], dy_ref[1], dx_ref[0], dx_ref[1], dx_ref[2], dx_ref[3],
    )
    total = own_ref[...].astype(F32)
    for k, block in enumerate(arrived):
        total += dot(one_hot(iota((ROWS, 32), 0) == send_ref[0, k : k + 1, :]), block)
    out_ref[...] = total[:, :D].astype(BF)
    grad_ref[...] = total[:, D:].astype(BF)


def sum1_body(own_ref, got_ref, *outs):
    for i in range(8):
        at = slice(48 * i, 48 * (i + 1))
        outs[i][...] = (
            own_ref[at, :COLS_A].astype(F32) + got_ref[at, :COLS_A].astype(F32)
        ).astype(BF)
    for i in range(4):
        at = slice(96 * i, 96 * (i + 1))
        outs[8 + i][...] = (
            own_ref[at, COLS_A:].astype(F32) + got_ref[at, COLS_A:].astype(F32)
        ).astype(BF)


def added(refs):
    total = refs[0][...].astype(F32)
    for ref in refs[1:]:
        total += ref[...].astype(F32)
    return total.astype(BF)


def cut(total, parts, rows, padded):
    shape = (parts * padded, total.shape[0])
    j = iota(shape, 0)
    wanted = jnp.where(j % padded < rows, j // padded * rows + j % padded, -1)
    return dot(one_hot(iota(shape, 1) == wanted), total)


def sum2_body(*refs):
    ins, outs = refs[:12], refs[12:]
    a = cut(added(ins[:8]), 4, 12, 16)
    for i in range(4):
        outs[i][...] = a[16 * i : 16 * (i + 1)].astype(BF)
    b = cut(added(ins[8:]), 8, 12, 16)
    for i in range(8):
        outs[4 + i][...] = b[16 * i : 16 * (i + 1)].astype(BF)


def sum3_body(*refs):
    ins, outs = refs[:12], refs[12:]
    a = cut(added(ins[:4]), 4, 3, 8)
    b = cut(added(ins[4:]), 4, 3, 8)
    for i in range(4):
        outs[i][:, :COLS_A] = a[8 * i : 8 * (i + 1)].astype(BF)
        outs[i][:, COLS_A:] = b[8 * i : 8 * (i + 1)].astype(BF)


def sum4_body(*refs):
    ins, (qkv_ref, out_ref, gain_ref) = refs[:4], refs[4:]
    total = ins[0][...].astype(F32)
    for ref in ins[1:]:
        total += ref[...].astype(F32)
    qkv_ref[...] = total[:3, : 3 * D]
    out_ref[...] = total[:3, 3 * D : 4 * D]
    gain_ref[...] = total[:3, 4 * D :]


def call(body, shapes, *args, scratch=(), smem=()):
    return pl.pallas_call(
        body,
        out_shape=[jax.ShapeDtypeStruct(shape, dtype) for shape, dtype in shapes],
        in_specs=[
            pl.BlockSpec(memory_space=pltpu.SMEM) if i in smem else VMEM for i in range(len(args))
        ],
        out_specs=[VMEM] * len(shapes),
        scratch_shapes=list(scratch),
        compiler_params=PARAMS,
    )(*args)


def on_device(tokens, norm_gain, w_qkv, w_out, send_rows, window_rows, grad_out):
    gain = norm_gain.reshape(1, D)
    me = jnp.stack([lax.axis_index(a) for a in AXES]).astype(jnp.int32)
    (blocks,) = call(pack_body, [((7, 32, WIDE), BF)], tokens, grad_out, send_rows)
    from_x = passed_along(blocks[3:7], "gx", 1)
    from_y = passed_along(jnp.stack([blocks[1], blocks[2], from_x[2], from_x[3]]), "gy", 1)
    from_z = passed_along(jnp.stack([blocks[0], from_y[1], from_x[1], from_y[3]]), "gz", 1)

    half = (384, COLS)
    slot = (SLOTS, D)
    own, sent, xs, gos, mixed, dn = call(
        main_body,
        [(half, BF), (half, BF), (slot, BF), (slot, BF), (slot, BF), (slot, BF)],
        me, tokens, grad_out, from_x, from_y, from_z, window_rows, gain, w_qkv, w_out,
        scratch=[
            pltpu.VMEM((SLOTS, WIDE), BF),
            pltpu.VMEM(slot, BF),
            pltpu.VMEM(slot, F32),
            pltpu.VMEM((SLOTS, 3 * D), BF),
            pltpu.VMEM(slot, BF),
            pltpu.VMEM((SLOTS, 3 * D), BF),
        ],
        smem=(0,),
    )

    got = crossed(sent, "gz", 1)
    parts = call(sum1_body, [((48, COLS_A), BF)] * 8 + [((96, COLS_B), BF)] * 4, own, got)
    a = [parts[0]] + [crossed(parts[i], "gx", i) for i in range(1, 8)]
    b = [parts[8]] + [crossed(parts[8 + i], "gy", i) for i in range(1, 4)]
    parts = call(sum2_body, [((16, COLS_A), BF)] * 4 + [((16, COLS_B), BF)] * 8, *a, *b)
    a = [parts[0]] + [crossed(parts[i], "gy", i) for i in range(1, 4)]
    b = [parts[4]] + [crossed(parts[4 + i], "gx", i) for i in range(1, 8)]
    parts = call(sum3_body, [((8, COLS), BF)] * 4, *a, *b)
    c = [parts[0]] + [crossed(parts[i], "gz", 2 * i) for i in range(1, 4)]
    grad_qkv, grad_proj, gain_rows = call(
        sum4_body, [((3, 3 * D), F32), ((3, D), F32), ((3, 128), F32)], *c
    )

    kept, back = call(
        back_body, [((ROWS, WIDE), BF), ((7, 32, WIDE), BF)],
        xs, gos, mixed, dn, window_rows, gain, w_out,
        scratch=[pltpu.VMEM((SLOTS, WIDE), BF)],
    )
    down_z = passed_along(jnp.stack([back[0], back[2], back[4], back[6]]), "gz", -1)
    down_y = passed_along(jnp.stack([back[1], down_z[1], back[5], down_z[3]]), "gy", -1)
    down_x = passed_along(jnp.stack([back[3], down_z[2], down_y[2], down_y[3]]), "gx", -1)
    block_out, grad_tokens = call(
        join_body, [((ROWS, D), BF), ((ROWS, D), BF)], kept, down_x, down_y, down_z, send_rows
    )
    return (block_out, grad_tokens, gain_rows[:, 0], grad_qkv, grad_proj)


def solution(mesh):
    spread = P(AXES, None)
    in_specs = (spread, P(), P(), P(), P(AXES, None, None), spread, spread)
    out_specs = (spread, spread, P(AXES), spread, spread)
    return jax.shard_map(
        on_device, mesh=mesh, in_specs=in_specs, out_specs=out_specs, check_vma=False
    )
```

```python
import jax
import jax.numpy as jnp
from jax import lax
from jax.experimental import pallas as pl
from jax.experimental.pallas import tpu as pltpu
from jax.sharding import PartitionSpec as P

D = 768
WCAP = 128
SLOTS = 512
ROWS = 256
WIDE = 2 * D
HALF = 512
COLS = 3 * D + 128
AXES = ("gx", "gy", "gz")
FIRST = ("gx", "gy", "gz")
SECOND = ("gy", "gz", "gx")
EPSILON = 1e-06
BIG_NEGATIVE = -1e30
BF = jnp.bfloat16
F32 = jnp.float32
NT = (((1,), (1,)), ((), ()))
TN = (((0,), (0,)), ((), ()))
VMEM = pl.BlockSpec(memory_space=pltpu.VMEM)


def dot(a, b):
    return jnp.dot(a, b, preferred_element_type=F32)


def iota(shape, dim):
    return lax.broadcasted_iota(jnp.int32, shape, dim)


def column(row):
    n = row.shape[1]
    spread = jnp.broadcast_to(row.astype(F32), (n, n))
    return jnp.sum(jnp.where(iota((n, n), 0) == iota((n, n), 1), spread, 0.0), axis=1, keepdims=True)


def one_hot(condition):
    return jnp.where(condition, 1.0, 0.0).astype(BF)


def passed_along(value, axis, steps):
    count = lax.axis_size(axis)
    initial, last = (max(0, -steps), min(count, count - steps))
    return lax.ppermute(value, axis, [(source, source + steps) for source in range(initial, last)])


def bit(k, axis):
    return k // (4, 2, 1)[AXES.index(axis)] % 2


def carried(blocks, axes, steps):
    at = {k: blocks[k - 1 : k] for k in range(1, 8)}
    stages = []
    for axis in axes:
        moving = [k for k in range(1, 8) if bit(k, axis)]
        moved = passed_along(jnp.concatenate([at[k] for k in moving]), axis, steps)
        for i, k in enumerate(moving):
            at[k] = moved[i : i + 1]
        stages.append(moved)
    return stages


def arrival(axes):
    for k in range(1, 8):
        stage = max(s for s, axis in enumerate(axes) if bit(k, axis))
        moving = [m for m in range(1, 8) if bit(m, axes[stage])]
        yield stage, moving.index(k)


def crossed(value, axis, mask):
    count = lax.axis_size(axis)
    return lax.ppermute(value, axis, [(source, source ^ mask) for source in range(count)])


def pack_body(tok_ref, go_ref, send_ref, *outs):
    chosen = [
        one_hot(iota((32, ROWS), 1).astype(F32) == column(send_ref[0, k : k + 1, :])) for k in range(7)
    ]
    chosen = jnp.concatenate(chosen, axis=0)
    for part, ref in enumerate((tok_ref, go_ref)):
        outs[part][...] = dot(chosen, ref[...]).astype(BF).reshape(7, 32, D)


def normalised(x):
    centred = x - jnp.mean(x, axis=-1, keepdims=True)
    inv_std = lax.rsqrt(jnp.mean(centred * centred, axis=-1, keepdims=True) + EPSILON)
    return centred * inv_std, inv_std


def first_row(gz, core, block):
    gx, gy, z_hi = block // 16, block % 16 // 4, block % 4
    return ((gx * 4 + gy) * 8 + ((z_hi * 2 + core) ^ gz)) * 3


def half_place(gz, core):
    j = iota((HALF, 1), 0)
    row = jnp.where(j % 4 < 3, first_row(gz, core, j // 4) + j % 4, -1)
    return iota((HALF, D), 1) == row


def half_sums(gz, core, normed, mixed, gos, dpacked_ref, out_ref):
    place = half_place(gz, core)
    turned = lax.dot_general(one_hot(place), normed, NT, preferred_element_type=F32).astype(BF)
    i = iota((384, 1), 0)
    picks = one_hot(iota((384, D), 1) == first_row(gz, core, i % 128) + i // 128)
    picks = lax.dot_general(picks, mixed, NT, preferred_element_type=F32).astype(BF)
    proj = dot(picks, gos).astype(BF)
    j = iota((HALF, 1), 0)
    widen = one_hot(iota((HALF, 128), 1) == jnp.where(j % 4 == 3, j // 4, -1))
    for g in range(3):
        at = slice(g * D, (g + 1) * D)
        total = dot(turned, dpacked_ref[:, at]) + dot(widen, proj[g * 128 : (g + 1) * 128])
        out_ref[:, at] = total.astype(BF)
    return place


def main_body(
    me_ref, tok_ref, go_ref, t_refs, g_refs, win_ref, gain_ref, wqkv_ref, wout_ref,
    snd_ref, xs_ref, gos_ref, normed_ref, mixed_ref, dpacked_ref,
    rows_ref, packed_ref, delta_ref,
):
    rows_ref[:ROWS, :D] = tok_ref[...]
    rows_ref[:ROWS, D:] = go_ref[...]
    for part, (refs, axes) in enumerate(((t_refs, FIRST), (g_refs, SECOND))):
        for k, (stage, i) in enumerate(arrival(axes)):
            rows_ref[ROWS + 32 * k : ROWS + 32 * (k + 1), part * D : (part + 1) * D] = refs[stage][i]
    rows_ref[480:, :] = jnp.zeros((32, WIDE), BF)
    gain = gain_ref[...]

    def gather_window(w, carry):
        at = pl.ds(pl.multiple_of(w * WCAP, WCAP), WCAP)
        picks = one_hot(iota((WCAP, SLOTS), 1).astype(F32) == column(win_ref[:, at]))
        taken = dot(picks, rows_ref[...])
        x = taken[:, :D]
        xs_ref[at, :] = x.astype(BF)
        gos_ref[at, :] = taken[:, D:].astype(BF)
        unit, _ = normalised(x)
        normed_ref[at, :] = (unit * gain).astype(BF)
        return carry

    lax.fori_loop(0, SLOTS // WCAP, gather_window, 0)

    def project(c, carry):
        at = pl.ds(pl.multiple_of(c * D, D), D)
        packed_ref[:, at] = dot(normed_ref[...], wqkv_ref[:, at]).astype(BF)
        return carry

    lax.fori_loop(0, 3, project, 0)
    delta_ref[...] = lax.dot_general(
        gos_ref[...], wout_ref[...], NT, preferred_element_type=F32
    ).astype(BF)

    low = iota((WCAP, 128), 1) < 64
    zero = jnp.zeros((), BF)

    def both(value):
        return jnp.concatenate([jnp.where(low, value, zero), jnp.where(low, zero, value)], axis=0)

    def attend(w, carry):
        at = pl.ds(pl.multiple_of(w * WCAP, WCAP), WCAP)
        filled = jnp.broadcast_to(column(win_ref[:, at]) >= 0, (WCAP, WCAP))[None]
        for p in range(6):
            q_at = pl.ds(p * 128, 128)
            k_at = pl.ds(D + p * 128, 128)
            v_at = pl.ds(2 * D + p * 128, 128)
            q = packed_ref[at, q_at]
            k_both = both(packed_ref[at, k_at])
            v_both = both(packed_ref[at, v_at])
            d = delta_ref[at, q_at]
            scores = lax.dot_general(k_both, q, NT, preferred_element_type=F32) * 0.125
            scores = jnp.where(filled, scores.reshape(2, WCAP, WCAP), BIG_NEGATIVE)
            expo = jnp.exp(scores - jnp.max(scores, axis=1, keepdims=True))
            probs = expo * (1.0 / jnp.sum(expo, axis=1, keepdims=True))
            weights = probs.astype(BF)
            mixed = lax.dot_general(
                weights.reshape(2 * WCAP, WCAP), v_both, TN, preferred_element_type=F32
            )
            mixed_ref[at, q_at] = mixed.astype(BF)
            dweights = lax.dot_general(v_both, d, NT, preferred_element_type=F32)
            dweights = dweights.reshape(2, WCAP, WCAP)
            inner = jnp.sum(dweights * probs, axis=1, keepdims=True)
            dscaled = (probs * (dweights - inner) * 0.125).astype(BF)
            dq = lax.dot_general(
                dscaled.reshape(2 * WCAP, WCAP), k_both, TN, preferred_element_type=F32
            )
            dpacked_ref[at, q_at] = dq.astype(BF)
            beside = jnp.concatenate([dscaled[0], dscaled[1]], axis=1)
            dpacked_ref[at, k_at] = dot(beside, both(q)).astype(BF)
            beside = jnp.concatenate([weights[0], weights[1]], axis=1)
            dpacked_ref[at, v_at] = dot(beside, both(d)).astype(BF)
        return carry

    lax.fori_loop(0, SLOTS // WCAP, attend, 0)

    half_sums(
        me_ref[0], 1, normed_ref[...], mixed_ref[...], gos_ref[...], dpacked_ref, snd_ref
    )


def back_body(
    me_ref, xs_ref, gos_ref, normed_ref, mixed_ref, dpacked_ref, win_ref, gain_ref, wqkv_ref, wout_ref,
    own_ref, gain_own_ref, gain_snd_ref, kept_ref, *rest,
):
    ret_refs, cat_ref, dn_ref = rest[:-2], rest[-2], rest[-1]
    gain = gain_ref[...]
    place = half_sums(
        me_ref[0], 0, normed_ref[...], mixed_ref[...], gos_ref[...], dpacked_ref, own_ref
    )
    dn_ref[...] = lax.dot_general(
        dpacked_ref[...], wqkv_ref[...], NT, preferred_element_type=F32
    ).astype(BF)
    gain_row = jnp.zeros((1, D), F32)
    projected = dot(mixed_ref[...], wout_ref[...])
    cat_ref[:, :D] = (xs_ref[...].astype(F32) + projected).astype(BF)
    for w in range(4):
        at = slice(w * WCAP, (w + 1) * WCAP)
        unit, inv_std = normalised(xs_ref[at, :].astype(F32))
        dnormed = dn_ref[at, :].astype(F32)
        gain_row += jnp.sum(dnormed * unit, axis=0, keepdims=True)
        dunit = dnormed * gain
        dcentre = inv_std * (
            dunit
            - jnp.mean(dunit, axis=-1, keepdims=True)
            - unit * jnp.mean(dunit * unit, axis=-1, keepdims=True)
        )
        cat_ref[at, D:] = (gos_ref[at, :].astype(F32) + dcentre).astype(BF)
    back = one_hot(iota((480, SLOTS), 0) == win_ref[...])
    kept_ref[...] = dot(back[:ROWS], cat_ref[...]).astype(BF)
    sent = dot(back[ROWS:], cat_ref[...]).astype(BF).reshape(7, 32, WIDE)
    for part, ref in enumerate(ret_refs):
        ref[...] = sent[:, :, part * D : (part + 1) * D]
    own = jnp.where(place, gain_row, 0.0)
    gain_own_ref[...] = jnp.broadcast_to(jnp.sum(own, axis=1, keepdims=True), (HALF, 128))
    other = half_place(me_ref[0], 1)
    own = jnp.where(other, gain_row, 0.0)
    gain_snd_ref[...] = jnp.broadcast_to(jnp.sum(own, axis=1, keepdims=True), (HALF, 128))


def join_body(kept_ref, t_refs, g_refs, send_ref, out_ref, grad_ref):
    for part, (refs, axes, out) in enumerate(
        ((t_refs, FIRST, out_ref), (g_refs, SECOND, grad_ref))
    ):
        total = kept_ref[:, part * D : (part + 1) * D].astype(F32)
        for k, (stage, i) in enumerate(arrival(axes[::-1])):
            total += dot(one_hot(iota((ROWS, 32), 0) == send_ref[0, k : k + 1, :]), refs[stage][i])
        out[...] = total.astype(BF)


def sum1_body(own_ref, got_ref, gain_own_ref, gain_got_ref, out_ref):
    out_ref[:, : 3 * D] = (own_ref[...].astype(F32) + got_ref[...].astype(F32)).astype(BF)
    out_ref[:, 3 * D :] = (gain_own_ref[...] + gain_got_ref[...]).astype(BF)


def sum2_body(got_ref, *outs):
    total = jnp.sum(got_ref[...].astype(F32), axis=0)
    for i in range(4):
        outs[i][...] = total[4 * i : 4 * (i + 1)].astype(BF)


def sum3_body(a_ref, b_ref, c_ref, d_ref, qkv_ref, out_ref, gain_ref):
    total = a_ref[...].astype(F32) + b_ref[...].astype(F32)
    total += c_ref[...].astype(F32) + d_ref[...].astype(F32)
    qkv_ref[...] = total[:3, : 3 * D]
    for g in range(3):
        out_ref[g : g + 1, :] = total[3:4, g * D : (g + 1) * D]
    gain_ref[...] = total[:3, 3 * D :]


def call(body, shapes, *args, scratch=(), smem=(), mib=16):
    tree = jax.tree.structure(args)
    count = tree.num_leaves

    def flat(*refs):
        body(*jax.tree.unflatten(tree, refs[:count]), *refs[count:])

    return pl.pallas_call(
        flat,
        out_shape=[jax.ShapeDtypeStruct(shape, dtype) for shape, dtype in shapes],
        in_specs=[pl.BlockSpec(memory_space=pltpu.SMEM) if i in smem else VMEM for i in range(count)],
        out_specs=[VMEM] * len(shapes),
        scratch_shapes=list(scratch),
        compiler_params=pltpu.CompilerParams(vmem_limit_bytes=mib * 1024 * 1024),
    )(*jax.tree.leaves(args))


def on_device(tokens, norm_gain, w_qkv, w_out, send_rows, window_rows, grad_out):
    gain = norm_gain.reshape(1, D)
    me = lax.axis_index("gz").astype(jnp.int32).reshape(1)
    lists = ((7, 32, D), BF)
    blocks = call(pack_body, [lists, lists], tokens, grad_out, send_rows)
    arrived_t = carried(blocks[0], FIRST, 1)
    arrived_g = carried(blocks[1], SECOND, 1)

    slot, wide, half = ((SLOTS, D), BF), ((SLOTS, 3 * D), BF), ((HALF, 3 * D), BF)
    gains = ((HALF, 128), F32)
    sent, xs, gos, normed, mixed, dpacked = call(
        main_body,
        [half, slot, slot, slot, slot, wide],
        me, tokens, grad_out, arrived_t, arrived_g, window_rows, gain, w_qkv, w_out,
        scratch=[pltpu.VMEM((SLOTS, WIDE), BF), pltpu.VMEM(*wide), pltpu.VMEM(*slot)],
        smem=(0,),
        mib=34,
    )
    got = crossed(sent, "gz", 1)
    own, gain_own, gain_sent, kept, *back = call(
        back_body,
        [half, gains, gains, ((ROWS, WIDE), BF), lists, lists],
        me, xs, gos, normed, mixed, dpacked, window_rows, gain, w_qkv, w_out,
        scratch=[pltpu.VMEM((SLOTS, WIDE), BF), pltpu.VMEM(*slot)],
        smem=(0,),
        mib=34,
    )
    gain_got = crossed(gain_sent, "gz", 1)

    (paired,) = call(sum1_body, [((HALF, COLS), BF)], own, got, gain_own, gain_got)
    spread = lax.all_to_all(paired, ("gx", "gy"), split_axis=0, concat_axis=0, tiled=True)
    parts = call(sum2_body, [((4, COLS), BF)] * 4, spread.reshape(32, 16, COLS))
    last = [parts[0]] + [crossed(parts[i], "gz", 2 * i) for i in range(1, 4)]
    grad_qkv, grad_proj, gain_rows = call(
        sum3_body, [((3, 3 * D), F32), ((3, D), F32), ((3, 128), F32)], *last
    )

    block_out, grad_tokens = call(
        join_body,
        [((ROWS, D), BF), ((ROWS, D), BF)],
        kept,
        carried(back[0], FIRST[::-1], -1),
        carried(back[1], SECOND[::-1], -1),
        send_rows,
    )
    return (block_out, grad_tokens, gain_rows[:, 0], grad_qkv, grad_proj)


def solution(mesh):
    spread = P(AXES, None)
    in_specs = (spread, P(), P(), P(), P(AXES, None, None), spread, spread)
    out_specs = (spread, spread, P(AXES), spread, spread)
    return jax.shard_map(
        on_device, mesh=mesh, in_specs=in_specs, out_specs=out_specs, check_vma=False
    )
```

```python
import functools

import jax
import jax.numpy as jnp
from jax import lax
from jax.experimental import pallas as pl
from jax.experimental.pallas import tpu as pltpu
from jax.sharding import PartitionSpec as P

D = 768
WCAP = 128
SLOTS = 512
ROWS = 256
WIDE = 2 * D
HALF = 512
MAIN, BACK, SUMS, SMALL = 18, 16, 12, 6
COLS = 3 * D + 128
AXES = ("gx", "gy", "gz")
FIRST = ("gx", "gy", "gz")
SECOND = ("gy", "gz", "gx")
EPSILON = 1e-06
BIG_NEGATIVE = -1e30
BF = jnp.bfloat16
F32 = jnp.float32
NT = (((1,), (1,)), ((), ()))
TN = (((0,), (0,)), ((), ()))
VMEM = pl.BlockSpec(memory_space=pltpu.VMEM)
SMEM = pl.BlockSpec(memory_space=pltpu.SMEM)
ANY = pl.BlockSpec(memory_space=pl.ANY)


def dot(a, b):
    return jnp.dot(a, b, preferred_element_type=F32)


def iota(shape, dim):
    return lax.broadcasted_iota(jnp.int32, shape, dim)


def column(row):
    n = row.shape[1]
    spread = jnp.broadcast_to(row.astype(F32), (n, n))
    return jnp.sum(jnp.where(iota((n, n), 0) == iota((n, n), 1), spread, 0.0), axis=1, keepdims=True)


def one_hot(condition):
    return jnp.where(condition, 1.0, 0.0).astype(BF)


def passed_along(value, axis, steps):
    count = lax.axis_size(axis)
    initial, last = (max(0, -steps), min(count, count - steps))
    return lax.ppermute(value, axis, [(source, source + steps) for source in range(initial, last)])


def bit(k, axis):
    return k // (4, 2, 1)[AXES.index(axis)] % 2


def stage(at, axis, steps):
    moving = [k for k in range(1, 8) if bit(k, axis)]
    moved = passed_along(jnp.concatenate([at[k] for k in moving]), axis, steps)
    return at | {k: moved[i : i + 1] for i, k in enumerate(moving)}, moved


def numbered(blocks):
    return {k: blocks[k - 1 : k] for k in range(1, 8)}


def carried(t, g, steps, ways):
    t, g = numbered(t), numbered(g)
    for axis_t, axis_g in zip(*ways):
        t, moved_t = stage(t, axis_t, steps)
        g, moved_g = stage(g, axis_g, steps)
        yield moved_t, moved_g


def arrival(axes):
    for k in range(1, 8):
        stage = max(s for s, axis in enumerate(axes) if bit(k, axis))
        moving = [m for m in range(1, 8) if bit(m, axes[stage])]
        yield stage, moving.index(k)


def crossed(value, axis, mask):
    count = lax.axis_size(axis)
    return lax.ppermute(value, axis, [(source, source ^ mask) for source in range(count)])


def named(send_ref):
    rows = [one_hot(iota((32, ROWS), 1).astype(F32) == column(send_ref[0, k : k + 1, :])) for k in range(7)]
    return jnp.concatenate(rows, axis=0)


def fetches(t_refs, g_refs, axes, to_ref, start, sems):
    copies = []
    for part, (refs, way) in enumerate(((t_refs, axes[0]), (g_refs, axes[1]))):
        for k, (stage, i) in enumerate(arrival(way)):
            at = to_ref.at[pl.ds(start + 32 * k, 32), pl.ds(part * D, D)]
            copies.append(pltpu.make_async_copy(refs[stage].at[i], at, sems.at[part, k]))
    return copies


def pack_body(tok_ref, go_ref, send_ref, *outs):
    chosen = named(send_ref)
    for part, ref in enumerate((tok_ref, go_ref)):
        outs[part][...] = dot(chosen, ref[...]).astype(BF).reshape(7, 32, D)


def normalised(x):
    centred = x - jnp.mean(x, axis=-1, keepdims=True)
    inv_std = lax.rsqrt(jnp.mean(centred * centred, axis=-1, keepdims=True) + EPSILON)
    return centred * inv_std, inv_std


def first_row(gz, core, block):
    gx, gy, z_hi = block // 16, block % 16 // 4, block % 4
    return ((gx * 4 + gy) * 8 + ((z_hi * 2 + core) ^ gz)) * 3


def half_place(gz, core):
    j = iota((HALF, 1), 0)
    row = jnp.where(j % 4 < 3, first_row(gz, core, j // 4) + j % 4, -1)
    return iota((HALF, D), 1) == row


def half_sums(core, me_ref, normed_ref, mixed_ref, gos_ref, dpacked_ref, gain_ref, out_ref):
    gz = me_ref[0]
    place = half_place(gz, core)
    turned = lax.dot_general(one_hot(place), normed_ref[...], NT, preferred_element_type=F32).astype(BF)
    i = iota((384, 1), 0)
    picks = one_hot(iota((384, D), 1) == first_row(gz, core, i % 128) + i // 128)
    picks = lax.dot_general(picks, mixed_ref[...], NT, preferred_element_type=F32).astype(BF)
    proj = dot(picks, gos_ref[...]).astype(BF)
    j = iota((HALF, 1), 0)
    widen = one_hot(iota((HALF, 128), 1) == jnp.where(j % 4 == 3, j // 4, -1))
    for g in range(3):
        at = slice(g * D, (g + 1) * D)
        total = dot(turned, dpacked_ref[:, at]) + dot(widen, proj[g * 128 : (g + 1) * 128])
        out_ref[:, at] = total.astype(BF)
    gains = jnp.sum(jnp.where(place, gain_ref[...], 0.0), axis=1, keepdims=True)
    out_ref[:, 3 * D :] = jnp.broadcast_to(gains, (HALF, 128)).astype(BF)


def main_body(
    tok_ref, go_ref, t_refs, g_refs, win_ref, gain_ref, wqkv_ref, wout_ref,
    xs_ref, gos_ref, normed_ref, mixed_ref, dpacked_ref,
    rows_ref, packed_ref, delta_ref, held_ref, sems,
):
    copies = fetches(t_refs, g_refs, (FIRST, SECOND), rows_ref, ROWS, sems)
    own = rows_ref.at[pl.ds(0, ROWS), :]
    copies.append(pltpu.make_async_copy(tok_ref, own.at[:, pl.ds(0, D)], sems.at[0, 7]))
    copies.append(pltpu.make_async_copy(go_ref, own.at[:, pl.ds(D, D)], sems.at[1, 7]))
    weights_copy = pltpu.make_async_copy(wout_ref, held_ref, sems.at[2, 0])
    for copy in copies:
        copy.start()
    weights_copy.start()
    rows_ref[480:, :] = jnp.zeros((32, WIDE), BF)
    gain = gain_ref[...]
    for copy in copies:
        copy.wait()

    def gather_window(w, carry):
        at = pl.ds(pl.multiple_of(w * WCAP, WCAP), WCAP)
        picks = one_hot(iota((WCAP, SLOTS), 1).astype(F32) == column(win_ref[:, at]))
        taken = dot(picks, rows_ref[...])
        x = taken[:, :D]
        xs_ref[at, :] = x.astype(BF)
        gos_ref[at, :] = taken[:, D:].astype(BF)
        unit, _ = normalised(x)
        normed_ref[at, :] = (unit * gain).astype(BF)
        return carry

    lax.fori_loop(0, SLOTS // WCAP, gather_window, 0)

    def project(c, carry):
        at = pl.ds(pl.multiple_of(c * D, D), D)
        packed_ref[:, at] = dot(normed_ref[...], wqkv_ref[:, at]).astype(BF)
        return carry

    lax.fori_loop(0, 3, project, 0)
    weights_copy.wait()
    delta_ref[...] = lax.dot_general(
        gos_ref[...], held_ref[...], NT, preferred_element_type=F32
    ).astype(BF)

    low = iota((WCAP, 128), 1) < 64
    zero = jnp.zeros((), BF)

    def both(value):
        return jnp.concatenate([jnp.where(low, value, zero), jnp.where(low, zero, value)], axis=0)

    def attend(w, carry):
        at = pl.ds(pl.multiple_of(w * WCAP, WCAP), WCAP)
        filled = jnp.broadcast_to(column(win_ref[:, at]) >= 0, (WCAP, WCAP))[None]
        for p in range(6):
            q_at = pl.ds(p * 128, 128)
            k_at = pl.ds(D + p * 128, 128)
            v_at = pl.ds(2 * D + p * 128, 128)
            q = packed_ref[at, q_at]
            k_both = both(packed_ref[at, k_at])
            v_both = both(packed_ref[at, v_at])
            d = delta_ref[at, q_at]
            scores = lax.dot_general(k_both, q, NT, preferred_element_type=F32) * 0.125
            scores = jnp.where(filled, scores.reshape(2, WCAP, WCAP), BIG_NEGATIVE)
            expo = jnp.exp(scores - jnp.max(scores, axis=1, keepdims=True))
            probs = expo * (1.0 / jnp.sum(expo, axis=1, keepdims=True))
            weights = probs.astype(BF)
            mixed = lax.dot_general(
                weights.reshape(2 * WCAP, WCAP), v_both, TN, preferred_element_type=F32
            )
            mixed_ref[at, q_at] = mixed.astype(BF)
            dweights = lax.dot_general(v_both, d, NT, preferred_element_type=F32)
            dweights = dweights.reshape(2, WCAP, WCAP)
            inner = jnp.sum(dweights * probs, axis=1, keepdims=True)
            dscaled = (probs * (dweights - inner) * 0.125).astype(BF)
            dq = lax.dot_general(
                dscaled.reshape(2 * WCAP, WCAP), k_both, TN, preferred_element_type=F32
            )
            dpacked_ref[at, q_at] = dq.astype(BF)
            beside = jnp.concatenate([dscaled[0], dscaled[1]], axis=1)
            dpacked_ref[at, k_at] = dot(beside, both(q)).astype(BF)
            beside = jnp.concatenate([weights[0], weights[1]], axis=1)
            dpacked_ref[at, v_at] = dot(beside, both(d)).astype(BF)
        return carry

    lax.fori_loop(0, SLOTS // WCAP, attend, 0)


def back_body(
    xs_ref, gos_ref, mixed_ref, dpacked_ref, win_ref, gain_ref, wqkv_ref, wout_ref,
    t_ref, g_ref, kept_ref, gain_sum_ref, cat_ref, dn_ref,
):
    gain = gain_ref[...]
    dn_ref[...] = lax.dot_general(
        dpacked_ref[...], wqkv_ref[...], NT, preferred_element_type=F32
    ).astype(BF)
    gain_row = jnp.zeros((1, D), F32)
    projected = dot(mixed_ref[...], wout_ref[...])
    cat_ref[:, :D] = (xs_ref[...].astype(F32) + projected).astype(BF)
    for w in range(4):
        at = slice(w * WCAP, (w + 1) * WCAP)
        unit, inv_std = normalised(xs_ref[at, :].astype(F32))
        dnormed = dn_ref[at, :].astype(F32)
        gain_row += jnp.sum(dnormed * unit, axis=0, keepdims=True)
        dunit = dnormed * gain
        dcentre = inv_std * (
            dunit
            - jnp.mean(dunit, axis=-1, keepdims=True)
            - unit * jnp.mean(dunit * unit, axis=-1, keepdims=True)
        )
        cat_ref[at, D:] = (gos_ref[at, :].astype(F32) + dcentre).astype(BF)
    back = one_hot(iota((480, SLOTS), 0) == win_ref[...])
    kept_ref[...] = dot(back[:ROWS], cat_ref[...]).astype(BF)
    sent = dot(back[ROWS:], cat_ref[...]).astype(BF).reshape(7, 32, WIDE)
    t_ref[...] = sent[:, :, :D]
    g_ref[...] = sent[:, :, D:]
    gain_sum_ref[...] = gain_row


def join_body(kept_ref, t_refs, g_refs, send_ref, out_ref, grad_ref, own_ref, rows_ref, sems):
    copies = fetches(t_refs, g_refs, (FIRST[::-1], SECOND[::-1]), rows_ref, 0, sems)
    copies.append(pltpu.make_async_copy(kept_ref, own_ref, sems.at[2, 0]))
    for copy in copies:
        copy.start()
    chosen = named(send_ref)
    for copy in copies:
        copy.wait()
    for part, out in enumerate((out_ref, grad_ref)):
        at = slice(part * D, (part + 1) * D)
        back = lax.dot_general(chosen, rows_ref[:, at], TN, preferred_element_type=F32)
        out[...] = (own_ref[:, at].astype(F32) + back).astype(BF)


def sum1_body(own_ref, got_ref, out_ref):
    out_ref[...] = (own_ref[...].astype(F32) + got_ref[...].astype(F32)).astype(BF)


def sum2_body(got_ref, *outs):
    total = jnp.sum(got_ref[...].astype(F32), axis=0)
    for i in range(4):
        outs[i][...] = total[4 * i : 4 * (i + 1)].astype(BF)


def sum3_body(a_ref, b_ref, c_ref, d_ref, qkv_ref, out_ref, gain_ref):
    total = a_ref[...].astype(F32) + b_ref[...].astype(F32)
    total += c_ref[...].astype(F32) + d_ref[...].astype(F32)
    qkv_ref[...] = total[:3, : 3 * D]
    for g in range(3):
        out_ref[g : g + 1, :] = total[3:4, g * D : (g + 1) * D]
    gain_ref[...] = total[:3, 3 * D :]


def call(body, shapes, *args, scratch=(), smem=(), outside=(), mib=SMALL):
    tree = jax.tree.structure(args)
    count = tree.num_leaves

    def flat(*refs):
        body(*jax.tree.unflatten(tree, refs[:count]), *refs[count:])

    return pl.pallas_call(
        flat,
        out_shape=[jax.ShapeDtypeStruct(shape, dtype) for shape, dtype in shapes],
        in_specs=[ANY if i in outside else SMEM if i in smem else VMEM for i in range(count)],
        out_specs=[VMEM] * len(shapes),
        scratch_shapes=list(scratch),
        compiler_params=pltpu.CompilerParams(vmem_limit_bytes=mib * 1024 * 1024),
    )(*jax.tree.leaves(args))


def on_device(tokens, norm_gain, w_qkv, w_out, send_rows, window_rows, grad_out):
    gain = norm_gain.reshape(1, D)
    me = lax.axis_index("gz").astype(jnp.int32).reshape(1)
    me, tokens, grad_out = lax.optimization_barrier((me, tokens, grad_out))
    lists = ((7, 32, D), BF)
    blocks = call(pack_body, [lists, lists], tokens, grad_out, send_rows)
    arrived_t, arrived_g = zip(*carried(*blocks, 1, (FIRST, SECOND)))

    slot, wide, half = ((SLOTS, D), BF), ((SLOTS, 3 * D), BF), ((HALF, COLS), BF)
    xs, gos, normed, mixed, dpacked = call(
        main_body,
        [slot, slot, slot, slot, wide],
        tokens, grad_out, arrived_t, arrived_g, window_rows, gain, w_qkv, w_out,
        scratch=[
            pltpu.VMEM((SLOTS, WIDE), BF),
            pltpu.VMEM(*wide),
            pltpu.VMEM(*slot),
            pltpu.VMEM((D, D), BF),
            pltpu.SemaphoreType.DMA((3, 8)),
        ],
        outside=(0, 1, 2, 3, 4, 5, 6, 7, 11),
        mib=MAIN,
    )
    back_t, back_g, kept, gain_sum = call(
        back_body,
        [lists, lists, ((ROWS, WIDE), BF), ((1, D), F32)],
        xs, gos, mixed, dpacked, window_rows, gain, w_qkv, w_out,
        scratch=[pltpu.VMEM((SLOTS, WIDE), BF), pltpu.VMEM(*slot)],
        mib=BACK,
    )
    way = carried(back_t, back_g, -1, (FIRST[::-1], SECOND[::-1]))
    first = next(way)
    operands = (me, normed, mixed, gos, dpacked, gain_sum)
    (sent,) = call(functools.partial(half_sums, 1), [half], *operands, smem=(0,), mib=SUMS)
    got = crossed(sent, "gz", 1)
    operands, first = lax.optimization_barrier((operands, first))
    (own,) = call(functools.partial(half_sums, 0), [half], *operands, smem=(0,), mib=SUMS)

    (paired,) = call(sum1_body, [half], own, got)
    second = next(way)
    paired, second = lax.optimization_barrier((paired, second))
    third = next(way)
    spread = lax.all_to_all(paired, ("gx", "gy"), split_axis=0, concat_axis=0, tiled=True)
    parts = call(sum2_body, [((4, COLS), BF)] * 4, spread.reshape(32, 16, COLS))
    last = [parts[0]] + [crossed(parts[i], "gz", 2 * i) for i in range(1, 4)]
    grad_qkv, grad_proj, gain_rows = call(
        sum3_body, [((3, 3 * D), F32), ((3, D), F32), ((3, 128), F32)], *last
    )

    block_out, grad_tokens = call(
        join_body,
        [((ROWS, D), BF), ((ROWS, D), BF)],
        kept, *zip(first, second, third), send_rows,
        scratch=[
            pltpu.VMEM((ROWS, WIDE), BF),
            pltpu.VMEM((224, WIDE), BF),
            pltpu.SemaphoreType.DMA((3, 8)),
        ],
        outside=range(7),
    )
    return (block_out, grad_tokens, gain_rows[:, 0], grad_qkv, grad_proj)


def solution(mesh):
    spread = P(AXES, None)
    in_specs = (spread, P(), P(), P(), P(AXES, None, None), spread, spread)
    out_specs = (spread, spread, P(AXES), spread, spread)
    return jax.shard_map(
        on_device, mesh=mesh, in_specs=in_specs, out_specs=out_specs, check_vma=False
    )
```

```python
import functools

import jax
import jax.numpy as jnp
from jax import lax
from jax.experimental import pallas as pl
from jax.experimental.pallas import tpu as pltpu
from jax.sharding import PartitionSpec as P

D = 768
WCAP = 128
SLOTS = 512
ROWS = 256
WIDE = 2 * D
HALF = 512
MAIN, BACK, SUMS, SMALL = 18, 16, 12, 6
COLS = 3 * D + 128
AXES = ("gx", "gy", "gz")
FIRST = ("gx", "gy", "gz")
SECOND = ("gy", "gz", "gx")
EPSILON = 1e-06
BIG_NEGATIVE = -1e30
BF = jnp.bfloat16
F32 = jnp.float32
NT = (((1,), (1,)), ((), ()))
TN = (((0,), (0,)), ((), ()))
VMEM = pl.BlockSpec(memory_space=pltpu.VMEM)
SMEM = pl.BlockSpec(memory_space=pltpu.SMEM)
ANY = pl.BlockSpec(memory_space=pl.ANY)


def dot(a, b):
    return jnp.dot(a, b, preferred_element_type=F32)


def iota(shape, dim):
    return lax.broadcasted_iota(jnp.int32, shape, dim)


def column(row):
    n = row.shape[1]
    spread = jnp.broadcast_to(row.astype(F32), (n, n))
    return jnp.sum(jnp.where(iota((n, n), 0) == iota((n, n), 1), spread, 0.0), axis=1, keepdims=True)


def one_hot(condition):
    return jnp.where(condition, 1.0, 0.0).astype(BF)


def passed_along(value, axis, steps):
    count = lax.axis_size(axis)
    initial, last = (max(0, -steps), min(count, count - steps))
    return lax.ppermute(value, axis, [(source, source + steps) for source in range(initial, last)])


def bit(k, axis):
    return k // (4, 2, 1)[AXES.index(axis)] % 2


def stage(arrays, place, axis, steps):
    moving = [k for k in range(1, 8) if bit(k, axis)]
    blocks = [lax.slice_in_dim(arrays[place[k][0]], place[k][1], place[k][1] + 1) for k in moving]
    for i, k in enumerate(moving):
        place[k] = (len(arrays), i)
    return [*arrays, passed_along(jnp.concatenate(blocks), axis, steps)]


def starts():
    return [{k: (0, k - 1) for k in range(1, 8)} for _ in range(2)]


def step(pair, places, ways, number, steps):
    return [
        stage(arrays, place, way[number], steps) for arrays, place, way in zip(pair, places, ways)
    ]


def arrival(axes):
    for k in range(1, 8):
        stage = max(s for s, axis in enumerate(axes) if bit(k, axis))
        moving = [m for m in range(1, 8) if bit(m, axes[stage])]
        yield stage, moving.index(k)


def crossed(value, axis, mask):
    count = lax.axis_size(axis)
    return lax.ppermute(value, axis, [(source, source ^ mask) for source in range(count)])


def named(send_ref):
    rows = [one_hot(iota((32, ROWS), 1).astype(F32) == column(send_ref[0, k : k + 1, :])) for k in range(7)]
    return jnp.concatenate(rows, axis=0)


def fetches(t_refs, g_refs, axes, to_ref, start, sems):
    copies = []
    for part, (refs, way) in enumerate(((t_refs, axes[0]), (g_refs, axes[1]))):
        for k, (stage, i) in enumerate(arrival(way)):
            at = to_ref.at[pl.ds(start + 32 * k, 32), pl.ds(part * D, D)]
            copies.append(pltpu.make_async_copy(refs[stage].at[i], at, sems.at[part, k]))
    return copies


def pack_body(tok_ref, go_ref, send_ref, *outs):
    chosen = named(send_ref)
    for part, ref in enumerate((tok_ref, go_ref)):
        outs[part][...] = dot(chosen, ref[...]).astype(BF).reshape(7, 32, D)


def normalised(x):
    centred = x - jnp.mean(x, axis=-1, keepdims=True)
    inv_std = lax.rsqrt(jnp.mean(centred * centred, axis=-1, keepdims=True) + EPSILON)
    return centred * inv_std, inv_std


def first_row(gz, core, block):
    gx, gy, z_hi = block // 16, block % 16 // 4, block % 4
    return ((gx * 4 + gy) * 8 + ((z_hi * 2 + core) ^ gz)) * 3


def half_place(gz, core):
    j = iota((HALF, 1), 0)
    row = jnp.where(j % 4 < 3, first_row(gz, core, j // 4) + j % 4, -1)
    return iota((HALF, D), 1) == row


def half_sums(core, me_ref, normed_ref, mixed_ref, gos_ref, dpacked_ref, gain_ref, out_ref):
    gz = me_ref[0]
    place = half_place(gz, core)
    turned = lax.dot_general(one_hot(place), normed_ref[...], NT, preferred_element_type=F32).astype(BF)
    i = iota((384, 1), 0)
    picks = one_hot(iota((384, D), 1) == first_row(gz, core, i % 128) + i // 128)
    picks = lax.dot_general(picks, mixed_ref[...], NT, preferred_element_type=F32).astype(BF)
    proj = dot(picks, gos_ref[...]).astype(BF)
    j = iota((HALF, 1), 0)
    widen = one_hot(iota((HALF, 128), 1) == jnp.where(j % 4 == 3, j // 4, -1))
    for g in range(3):
        at = slice(g * D, (g + 1) * D)
        total = dot(turned, dpacked_ref[:, at]) + dot(widen, proj[g * 128 : (g + 1) * 128])
        out_ref[:, at] = total.astype(BF)
    gains = jnp.sum(jnp.where(place, gain_ref[...], 0.0), axis=1, keepdims=True)
    out_ref[:, 3 * D :] = jnp.broadcast_to(gains, (HALF, 128)).astype(BF)


def main_body(
    tok_ref, go_ref, t_refs, g_refs, win_ref, gain_ref, wqkv_ref, wout_ref,
    xs_ref, gos_ref, normed_ref, mixed_ref, dpacked_ref,
    rows_ref, packed_ref, delta_ref, held_ref, sems,
):
    copies = fetches(t_refs, g_refs, (FIRST, SECOND), rows_ref, ROWS, sems)
    own = rows_ref.at[pl.ds(0, ROWS), :]
    copies.append(pltpu.make_async_copy(tok_ref, own.at[:, pl.ds(0, D)], sems.at[0, 7]))
    copies.append(pltpu.make_async_copy(go_ref, own.at[:, pl.ds(D, D)], sems.at[1, 7]))
    weights_copy = pltpu.make_async_copy(wout_ref, held_ref, sems.at[2, 0])
    for copy in copies:
        copy.start()
    weights_copy.start()
    rows_ref[480:, :] = jnp.zeros((32, WIDE), BF)
    gain = gain_ref[...]
    for copy in copies:
        copy.wait()

    def gather_window(w, carry):
        at = pl.ds(pl.multiple_of(w * WCAP, WCAP), WCAP)
        picks = one_hot(iota((WCAP, SLOTS), 1).astype(F32) == column(win_ref[:, at]))
        taken = dot(picks, rows_ref[...])
        x = taken[:, :D]
        xs_ref[at, :] = x.astype(BF)
        gos_ref[at, :] = taken[:, D:].astype(BF)
        unit, _ = normalised(x)
        normed_ref[at, :] = (unit * gain).astype(BF)
        return carry

    lax.fori_loop(0, SLOTS // WCAP, gather_window, 0)

    def project(c, carry):
        at = pl.ds(pl.multiple_of(c * D, D), D)
        packed_ref[:, at] = dot(normed_ref[...], wqkv_ref[:, at]).astype(BF)
        return carry

    lax.fori_loop(0, 3, project, 0)
    weights_copy.wait()
    delta_ref[...] = lax.dot_general(
        gos_ref[...], held_ref[...], NT, preferred_element_type=F32
    ).astype(BF)

    low = iota((WCAP, 128), 1) < 64
    zero = jnp.zeros((), BF)

    def both(value):
        return jnp.concatenate([jnp.where(low, value, zero), jnp.where(low, zero, value)], axis=0)

    def attend(w, carry):
        at = pl.ds(pl.multiple_of(w * WCAP, WCAP), WCAP)
        filled = jnp.broadcast_to(column(win_ref[:, at]) >= 0, (WCAP, WCAP))[None]
        for p in range(6):
            q_at = pl.ds(p * 128, 128)
            k_at = pl.ds(D + p * 128, 128)
            v_at = pl.ds(2 * D + p * 128, 128)
            q = packed_ref[at, q_at]
            k_both = both(packed_ref[at, k_at])
            v_both = both(packed_ref[at, v_at])
            d = delta_ref[at, q_at]
            scores = lax.dot_general(k_both, q, NT, preferred_element_type=F32) * 0.125
            scores = jnp.where(filled, scores.reshape(2, WCAP, WCAP), BIG_NEGATIVE)
            expo = jnp.exp(scores - jnp.max(scores, axis=1, keepdims=True))
            probs = expo * (1.0 / jnp.sum(expo, axis=1, keepdims=True))
            weights = probs.astype(BF)
            mixed = lax.dot_general(
                weights.reshape(2 * WCAP, WCAP), v_both, TN, preferred_element_type=F32
            )
            mixed_ref[at, q_at] = mixed.astype(BF)
            dweights = lax.dot_general(v_both, d, NT, preferred_element_type=F32)
            dweights = dweights.reshape(2, WCAP, WCAP)
            inner = jnp.sum(dweights * probs, axis=1, keepdims=True)
            dscaled = (probs * (dweights - inner) * 0.125).astype(BF)
            dq = lax.dot_general(
                dscaled.reshape(2 * WCAP, WCAP), k_both, TN, preferred_element_type=F32
            )
            dpacked_ref[at, q_at] = dq.astype(BF)
            beside = jnp.concatenate([dscaled[0], dscaled[1]], axis=1)
            dpacked_ref[at, k_at] = dot(beside, both(q)).astype(BF)
            beside = jnp.concatenate([weights[0], weights[1]], axis=1)
            dpacked_ref[at, v_at] = dot(beside, both(d)).astype(BF)
        return carry

    lax.fori_loop(0, SLOTS // WCAP, attend, 0)


def back_body(
    xs_ref, gos_ref, mixed_ref, dpacked_ref, win_ref, gain_ref, wqkv_ref, wout_ref,
    t_ref, g_ref, kept_ref, gain_sum_ref, cat_ref, dn_ref,
):
    gain = gain_ref[...]
    dn_ref[...] = lax.dot_general(
        dpacked_ref[...], wqkv_ref[...], NT, preferred_element_type=F32
    ).astype(BF)
    gain_row = jnp.zeros((1, D), F32)
    projected = dot(mixed_ref[...], wout_ref[...])
    cat_ref[:, :D] = (xs_ref[...].astype(F32) + projected).astype(BF)
    for w in range(4):
        at = slice(w * WCAP, (w + 1) * WCAP)
        unit, inv_std = normalised(xs_ref[at, :].astype(F32))
        dnormed = dn_ref[at, :].astype(F32)
        gain_row += jnp.sum(dnormed * unit, axis=0, keepdims=True)
        dunit = dnormed * gain
        dcentre = inv_std * (
            dunit
            - jnp.mean(dunit, axis=-1, keepdims=True)
            - unit * jnp.mean(dunit * unit, axis=-1, keepdims=True)
        )
        cat_ref[at, D:] = (gos_ref[at, :].astype(F32) + dcentre).astype(BF)
    back = one_hot(iota((480, SLOTS), 0) == win_ref[...])
    kept_ref[...] = dot(back[:ROWS], cat_ref[...]).astype(BF)
    sent = dot(back[ROWS:], cat_ref[...]).astype(BF).reshape(7, 32, WIDE)
    t_ref[...] = sent[:, :, :D]
    g_ref[...] = sent[:, :, D:]
    gain_sum_ref[...] = gain_row


def join_body(kept_ref, t_refs, g_refs, send_ref, out_ref, grad_ref, own_ref, rows_ref, sems):
    copies = fetches(t_refs, g_refs, (FIRST[::-1], SECOND[::-1]), rows_ref, 0, sems)
    copies.append(pltpu.make_async_copy(kept_ref, own_ref, sems.at[2, 0]))
    for copy in copies:
        copy.start()
    chosen = named(send_ref)
    for copy in copies:
        copy.wait()
    for part, out in enumerate((out_ref, grad_ref)):
        at = slice(part * D, (part + 1) * D)
        back = lax.dot_general(chosen, rows_ref[:, at], TN, preferred_element_type=F32)
        out[...] = (own_ref[:, at].astype(F32) + back).astype(BF)


def sum1_body(own_ref, got_ref, out_ref):
    out_ref[...] = (own_ref[...].astype(F32) + got_ref[...].astype(F32)).astype(BF)


def sum2_body(got_ref, *outs):
    total = jnp.sum(got_ref[...].astype(F32), axis=0)
    for i in range(4):
        outs[i][...] = total[4 * i : 4 * (i + 1)].astype(BF)


def sum3_body(a_ref, b_ref, c_ref, d_ref, qkv_ref, out_ref, gain_ref):
    total = a_ref[...].astype(F32) + b_ref[...].astype(F32)
    total += c_ref[...].astype(F32) + d_ref[...].astype(F32)
    qkv_ref[...] = total[:3, : 3 * D]
    for g in range(3):
        out_ref[g : g + 1, :] = total[3:4, g * D : (g + 1) * D]
    gain_ref[...] = total[:3, 3 * D :]


def call(body, shapes, *args, scratch=(), smem=(), outside=(), mib=SMALL):
    tree = jax.tree.structure(args)
    count = tree.num_leaves

    def flat(*refs):
        body(*jax.tree.unflatten(tree, refs[:count]), *refs[count:])

    return pl.pallas_call(
        flat,
        out_shape=[jax.ShapeDtypeStruct(shape, dtype) for shape, dtype in shapes],
        in_specs=[ANY if i in outside else SMEM if i in smem else VMEM for i in range(count)],
        out_specs=[VMEM] * len(shapes),
        scratch_shapes=list(scratch),
        compiler_params=pltpu.CompilerParams(vmem_limit_bytes=mib * 1024 * 1024),
    )(*jax.tree.leaves(args))


def on_device(tokens, norm_gain, w_qkv, w_out, send_rows, window_rows, grad_out):
    gain = norm_gain.reshape(1, D)
    me = lax.axis_index("gz").astype(jnp.int32).reshape(1)
    me, tokens, grad_out = lax.optimization_barrier((me, tokens, grad_out))
    lists = ((7, 32, D), BF)
    blocks = call(pack_body, [lists, lists], tokens, grad_out, send_rows)
    up = [[blocks[0]], [blocks[1]]]
    places = starts()
    for number in range(3):
        up = step(up, places, (FIRST, SECOND), number, 1)
    arrived_t, arrived_g = up[0][1:], up[1][1:]

    slot, wide, half = ((SLOTS, D), BF), ((SLOTS, 3 * D), BF), ((HALF, COLS), BF)
    xs, gos, normed, mixed, dpacked = call(
        main_body,
        [slot, slot, slot, slot, wide],
        tokens, grad_out, arrived_t, arrived_g, window_rows, gain, w_qkv, w_out,
        scratch=[
            pltpu.VMEM((SLOTS, WIDE), BF),
            pltpu.VMEM(*wide),
            pltpu.VMEM(*slot),
            pltpu.VMEM((D, D), BF),
            pltpu.SemaphoreType.DMA((3, 8)),
        ],
        outside=(0, 1, 2, 3, 4, 5, 6, 7, 11),
        mib=MAIN,
    )
    back_t, back_g, kept, gain_sum = call(
        back_body,
        [lists, lists, ((ROWS, WIDE), BF), ((1, D), F32)],
        xs, gos, mixed, dpacked, window_rows, gain, w_qkv, w_out,
        scratch=[pltpu.VMEM((SLOTS, WIDE), BF), pltpu.VMEM(*slot)],
        mib=BACK,
    )
    ways, places = (FIRST[::-1], SECOND[::-1]), starts()
    down = step([[back_t], [back_g]], places, ways, 0, -1)
    operands = (me, normed, mixed, gos, dpacked, gain_sum)
    (sent,) = call(functools.partial(half_sums, 1), [half], *operands, smem=(0,), mib=SUMS)
    got = crossed(sent, "gz", 1)
    (own,) = call(functools.partial(half_sums, 0), [half], *operands, smem=(0,), mib=SUMS)

    (paired,) = call(sum1_body, [half], own, got)
    paired, down = lax.optimization_barrier((paired, down))
    spread = lax.all_to_all(paired, ("gx", "gy"), split_axis=0, concat_axis=0, tiled=True)
    parts = call(sum2_body, [((4, COLS), BF)] * 4, spread.reshape(32, 16, COLS))
    parts, down = lax.optimization_barrier((parts, down))
    down = step(down, places, ways, 1, -1)
    last = [parts[0]] + [crossed(parts[i], "gz", 2 * i) for i in range(1, 4)]
    last, down = lax.optimization_barrier((last, down))
    down = step(down, places, ways, 2, -1)
    grad_qkv, grad_proj, gain_rows = call(
        sum3_body, [((3, 3 * D), F32), ((3, D), F32), ((3, 128), F32)], *last
    )

    block_out, grad_tokens = call(
        join_body,
        [((ROWS, D), BF), ((ROWS, D), BF)],
        kept, down[0][1:], down[1][1:], send_rows,
        scratch=[
            pltpu.VMEM((ROWS, WIDE), BF),
            pltpu.VMEM((224, WIDE), BF),
            pltpu.SemaphoreType.DMA((3, 8)),
        ],
        outside=range(7),
    )
    return (block_out, grad_tokens, gain_rows[:, 0], grad_qkv, grad_proj)


def solution(mesh):
    spread = P(AXES, None)
    in_specs = (spread, P(), P(), P(), P(AXES, None, None), spread, spread)
    out_specs = (spread, spread, P(AXES), spread, spread)
    return jax.shard_map(
        on_device, mesh=mesh, in_specs=in_specs, out_specs=out_specs, check_vma=False
    )
```

```python
import functools

import jax
import jax.numpy as jnp
from jax import lax
from jax.experimental import pallas as pl
from jax.experimental.pallas import tpu as pltpu
from jax.sharding import PartitionSpec as P

D = 768
WCAP = 128
SLOTS = 512
ROWS = 256
WIDE = 2 * D
HALF = 512
MAIN, BACK, SUMS, SMALL = 18, 16, 12, 6
COLS = 3 * D + 128
AXES = ("gx", "gy", "gz")
FIRST = ("gx", "gy", "gz")
SECOND = ("gy", "gz", "gx")
EPSILON = 1e-06
BIG_NEGATIVE = -1e30
BF = jnp.bfloat16
F32 = jnp.float32
NT = (((1,), (1,)), ((), ()))
TN = (((0,), (0,)), ((), ()))
VMEM = pl.BlockSpec(memory_space=pltpu.VMEM)
SMEM = pl.BlockSpec(memory_space=pltpu.SMEM)
ANY = pl.BlockSpec(memory_space=pl.ANY)


def dot(a, b):
    return jnp.dot(a, b, preferred_element_type=F32)


def iota(shape, dim):
    return lax.broadcasted_iota(jnp.int32, shape, dim)


def column(row):
    n = row.shape[1]
    spread = jnp.broadcast_to(row.astype(F32), (n, n))
    return jnp.sum(jnp.where(iota((n, n), 0) == iota((n, n), 1), spread, 0.0), axis=1, keepdims=True)


def one_hot(condition):
    return jnp.where(condition, 1.0, 0.0).astype(BF)


def passed_along(value, axis, steps):
    count = lax.axis_size(axis)
    initial, last = (max(0, -steps), min(count, count - steps))
    return lax.ppermute(value, axis, [(source, source + steps) for source in range(initial, last)])


def bit(k, axis):
    return k // (4, 2, 1)[AXES.index(axis)] % 2


def stage(arrays, place, axis, steps):
    moving = [k for k in range(1, 8) if bit(k, axis)]
    blocks = [lax.slice_in_dim(arrays[place[k][0]], place[k][1], place[k][1] + 1) for k in moving]
    for i, k in enumerate(moving):
        place[k] = (len(arrays), i)
    return [*arrays, passed_along(jnp.concatenate(blocks), axis, steps)]


def starts():
    return [{k: (0, k - 1) for k in range(1, 8)} for _ in range(2)]


def step(pair, places, ways, number, steps):
    return [
        stage(arrays, place, way[number], steps) for arrays, place, way in zip(pair, places, ways)
    ]


def arrival(axes):
    for k in range(1, 8):
        stage = max(s for s, axis in enumerate(axes) if bit(k, axis))
        moving = [m for m in range(1, 8) if bit(m, axes[stage])]
        yield stage, moving.index(k)


def crossed(value, axis, mask):
    count = lax.axis_size(axis)
    return lax.ppermute(value, axis, [(source, source ^ mask) for source in range(count)])


def named(send_ref):
    rows = [one_hot(iota((32, ROWS), 1).astype(F32) == column(send_ref[0, k : k + 1, :])) for k in range(7)]
    return jnp.concatenate(rows, axis=0)


def fetches(t_refs, g_refs, axes, to_ref, start, sems):
    copies = []
    for part, (refs, way) in enumerate(((t_refs, axes[0]), (g_refs, axes[1]))):
        for k, (stage, i) in enumerate(arrival(way)):
            at = to_ref.at[pl.ds(start + 32 * k, 32), pl.ds(part * D, D)]
            copies.append(pltpu.make_async_copy(refs[stage].at[i], at, sems.at[part, k]))
    return copies


def pack_body(tok_ref, go_ref, send_ref, *outs):
    chosen = named(send_ref)
    for part, ref in enumerate((tok_ref, go_ref)):
        outs[part][...] = dot(chosen, ref[...]).astype(BF).reshape(7, 32, D)


def normalised(x):
    centred = x - jnp.mean(x, axis=-1, keepdims=True)
    inv_std = lax.rsqrt(jnp.mean(centred * centred, axis=-1, keepdims=True) + EPSILON)
    return centred * inv_std, inv_std


def first_row(gz, core, block):
    gx, gy, z_hi = block // 16, block % 16 // 4, block % 4
    return ((gx * 4 + gy) * 8 + ((z_hi * 2 + core) ^ gz)) * 3


def half_place(gz, core):
    j = iota((HALF, 1), 0)
    row = jnp.where(j % 4 < 3, first_row(gz, core, j // 4) + j % 4, -1)
    return iota((HALF, D), 1) == row


def half_sums(core, me_ref, normed_ref, mixed_ref, gos_ref, dpacked_ref, gain_ref, out_ref):
    gz = me_ref[0]
    place = half_place(gz, core)
    turned = lax.dot_general(one_hot(place), normed_ref[...], NT, preferred_element_type=F32).astype(BF)
    i = iota((384, 1), 0)
    picks = one_hot(iota((384, D), 1) == first_row(gz, core, i % 128) + i // 128)
    picks = lax.dot_general(picks, mixed_ref[...], NT, preferred_element_type=F32).astype(BF)
    proj = dot(picks, gos_ref[...]).astype(BF)
    j = iota((HALF, 1), 0)
    widen = one_hot(iota((HALF, 128), 1) == jnp.where(j % 4 == 3, j // 4, -1))
    for g in range(3):
        at = slice(g * D, (g + 1) * D)
        total = dot(turned, dpacked_ref[:, at]) + dot(widen, proj[g * 128 : (g + 1) * 128])
        out_ref[:, at] = total.astype(BF)
    gains = jnp.sum(jnp.where(place, gain_ref[...], 0.0), axis=1, keepdims=True)
    out_ref[:, 3 * D :] = jnp.broadcast_to(gains, (HALF, 128)).astype(BF)


def main_body(
    tok_ref, go_ref, t_refs, g_refs, win_ref, gain_ref, wqkv_ref, wout_ref,
    xs_ref, gos_ref, normed_ref, mixed_ref, dpacked_ref, dn_ref, gain_sum_ref,
    rows_ref, packed_ref, delta_ref, held_ref, sems,
):
    copies = fetches(t_refs, g_refs, (FIRST, SECOND), rows_ref, ROWS, sems)
    own = rows_ref.at[pl.ds(0, ROWS), :]
    copies.append(pltpu.make_async_copy(tok_ref, own.at[:, pl.ds(0, D)], sems.at[0, 7]))
    copies.append(pltpu.make_async_copy(go_ref, own.at[:, pl.ds(D, D)], sems.at[1, 7]))
    weights_copy = pltpu.make_async_copy(wout_ref, held_ref, sems.at[2, 0])
    for copy in copies:
        copy.start()
    weights_copy.start()
    rows_ref[480:, :] = jnp.zeros((32, WIDE), BF)
    gain = gain_ref[...]
    for copy in copies:
        copy.wait()

    def gather_window(w, carry):
        at = pl.ds(pl.multiple_of(w * WCAP, WCAP), WCAP)
        picks = one_hot(iota((WCAP, SLOTS), 1).astype(F32) == column(win_ref[:, at]))
        taken = dot(picks, rows_ref[...])
        x = taken[:, :D]
        xs_ref[at, :] = x.astype(BF)
        gos_ref[at, :] = taken[:, D:].astype(BF)
        unit, _ = normalised(x)
        normed_ref[at, :] = (unit * gain).astype(BF)
        return carry

    lax.fori_loop(0, SLOTS // WCAP, gather_window, 0)

    def project(c, carry):
        at = pl.ds(pl.multiple_of(c * D, D), D)
        packed_ref[:, at] = dot(normed_ref[...], wqkv_ref[:, at]).astype(BF)
        return carry

    lax.fori_loop(0, 3, project, 0)
    weights_copy.wait()
    delta_ref[...] = lax.dot_general(
        gos_ref[...], held_ref[...], NT, preferred_element_type=F32
    ).astype(BF)

    low = iota((WCAP, 128), 1) < 64
    zero = jnp.zeros((), BF)

    def both(value):
        return jnp.concatenate([jnp.where(low, value, zero), jnp.where(low, zero, value)], axis=0)

    def attend(w, carry):
        at = pl.ds(pl.multiple_of(w * WCAP, WCAP), WCAP)
        filled = jnp.broadcast_to(column(win_ref[:, at]) >= 0, (WCAP, WCAP))[None]
        for p in range(6):
            q_at = pl.ds(p * 128, 128)
            k_at = pl.ds(D + p * 128, 128)
            v_at = pl.ds(2 * D + p * 128, 128)
            q = packed_ref[at, q_at]
            k_both = both(packed_ref[at, k_at])
            v_both = both(packed_ref[at, v_at])
            d = delta_ref[at, q_at]
            scores = lax.dot_general(k_both, q, NT, preferred_element_type=F32) * 0.125
            scores = jnp.where(filled, scores.reshape(2, WCAP, WCAP), BIG_NEGATIVE)
            expo = jnp.exp(scores - jnp.max(scores, axis=1, keepdims=True))
            probs = expo * (1.0 / jnp.sum(expo, axis=1, keepdims=True))
            weights = probs.astype(BF)
            mixed = lax.dot_general(
                weights.reshape(2 * WCAP, WCAP), v_both, TN, preferred_element_type=F32
            )
            mixed_ref[at, q_at] = mixed.astype(BF)
            dweights = lax.dot_general(v_both, d, NT, preferred_element_type=F32)
            dweights = dweights.reshape(2, WCAP, WCAP)
            inner = jnp.sum(dweights * probs, axis=1, keepdims=True)
            dscaled = (probs * (dweights - inner) * 0.125).astype(BF)
            dq = lax.dot_general(
                dscaled.reshape(2 * WCAP, WCAP), k_both, TN, preferred_element_type=F32
            )
            dpacked_ref[at, q_at] = dq.astype(BF)
            beside = jnp.concatenate([dscaled[0], dscaled[1]], axis=1)
            dpacked_ref[at, k_at] = dot(beside, both(q)).astype(BF)
            beside = jnp.concatenate([weights[0], weights[1]], axis=1)
            dpacked_ref[at, v_at] = dot(beside, both(d)).astype(BF)
        return carry

    lax.fori_loop(0, SLOTS // WCAP, attend, 0)
    dnormed = lax.dot_general(
        dpacked_ref[...], wqkv_ref[...], NT, preferred_element_type=F32
    ).astype(BF)
    dn_ref[...] = dnormed
    unit, _ = normalised(xs_ref[...].astype(F32))
    gain_sum_ref[...] = jnp.sum(dnormed.astype(F32) * unit, axis=0, keepdims=True)


def back_body(
    xs_ref, gos_ref, mixed_ref, dn_ref, win_ref, gain_ref, wout_ref, t_ref, g_ref, kept_ref, cat_ref,
):
    gain = gain_ref[...]
    projected = dot(mixed_ref[...], wout_ref[...])
    cat_ref[:, :D] = (xs_ref[...].astype(F32) + projected).astype(BF)
    for w in range(4):
        at = slice(w * WCAP, (w + 1) * WCAP)
        unit, inv_std = normalised(xs_ref[at, :].astype(F32))
        dnormed = dn_ref[at, :].astype(F32)
        dunit = dnormed * gain
        dcentre = inv_std * (
            dunit
            - jnp.mean(dunit, axis=-1, keepdims=True)
            - unit * jnp.mean(dunit * unit, axis=-1, keepdims=True)
        )
        cat_ref[at, D:] = (gos_ref[at, :].astype(F32) + dcentre).astype(BF)
    back = one_hot(iota((480, SLOTS), 0) == win_ref[...])
    kept_ref[...] = dot(back[:ROWS], cat_ref[...]).astype(BF)
    sent = dot(back[ROWS:], cat_ref[...]).astype(BF).reshape(7, 32, WIDE)
    t_ref[...] = sent[:, :, :D]
    g_ref[...] = sent[:, :, D:]


def join_body(kept_ref, t_refs, g_refs, send_ref, out_ref, grad_ref, own_ref, rows_ref, sems):
    copies = fetches(t_refs, g_refs, (FIRST[::-1], SECOND[::-1]), rows_ref, 0, sems)
    copies.append(pltpu.make_async_copy(kept_ref, own_ref, sems.at[2, 0]))
    for copy in copies:
        copy.start()
    chosen = named(send_ref)
    for copy in copies:
        copy.wait()
    for part, out in enumerate((out_ref, grad_ref)):
        at = slice(part * D, (part + 1) * D)
        back = lax.dot_general(chosen, rows_ref[:, at], TN, preferred_element_type=F32)
        out[...] = (own_ref[:, at].astype(F32) + back).astype(BF)


def sum1_body(own_ref, got_ref, out_ref):
    out_ref[...] = (own_ref[...].astype(F32) + got_ref[...].astype(F32)).astype(BF)


def sum2_body(got_ref, *outs):
    total = jnp.sum(got_ref[...].astype(F32), axis=0)
    for i in range(4):
        outs[i][...] = total[4 * i : 4 * (i + 1)].astype(BF)


def sum3_body(a_ref, b_ref, c_ref, d_ref, qkv_ref, out_ref, gain_ref):
    total = a_ref[...].astype(F32) + b_ref[...].astype(F32)
    total += c_ref[...].astype(F32) + d_ref[...].astype(F32)
    qkv_ref[...] = total[:3, : 3 * D]
    for g in range(3):
        out_ref[g : g + 1, :] = total[3:4, g * D : (g + 1) * D]
    gain_ref[...] = total[:3, 3 * D :]


def call(body, shapes, *args, scratch=(), smem=(), outside=(), mib=SMALL):
    tree = jax.tree.structure(args)
    count = tree.num_leaves

    def flat(*refs):
        body(*jax.tree.unflatten(tree, refs[:count]), *refs[count:])

    return pl.pallas_call(
        flat,
        out_shape=[jax.ShapeDtypeStruct(shape, dtype) for shape, dtype in shapes],
        in_specs=[ANY if i in outside else SMEM if i in smem else VMEM for i in range(count)],
        out_specs=[VMEM] * len(shapes),
        scratch_shapes=list(scratch),
        compiler_params=pltpu.CompilerParams(vmem_limit_bytes=mib * 1024 * 1024),
    )(*jax.tree.leaves(args))


def on_device(tokens, norm_gain, w_qkv, w_out, send_rows, window_rows, grad_out):
    gain = norm_gain.reshape(1, D)
    me = lax.axis_index("gz").astype(jnp.int32).reshape(1)
    me, tokens, grad_out = lax.optimization_barrier((me, tokens, grad_out))
    lists = ((7, 32, D), BF)
    blocks = call(pack_body, [lists, lists], tokens, grad_out, send_rows)
    up = [[blocks[0]], [blocks[1]]]
    places = starts()
    for number in range(3):
        up = step(up, places, (FIRST, SECOND), number, 1)
    arrived_t, arrived_g = up[0][1:], up[1][1:]

    slot, wide, half = ((SLOTS, D), BF), ((SLOTS, 3 * D), BF), ((HALF, COLS), BF)
    xs, gos, normed, mixed, dpacked, dn, gain_sum = call(
        main_body,
        [slot, slot, slot, slot, wide, slot, ((1, D), F32)],
        tokens, grad_out, arrived_t, arrived_g, window_rows, gain, w_qkv, w_out,
        scratch=[
            pltpu.VMEM((SLOTS, WIDE), BF),
            pltpu.VMEM(*wide),
            pltpu.VMEM(*slot),
            pltpu.VMEM((D, D), BF),
            pltpu.SemaphoreType.DMA((3, 8)),
        ],
        outside=(0, 1, 2, 3, 4, 5, 6, 7, 11),
        mib=MAIN,
    )
    operands = (me, normed, mixed, gos, dpacked, gain_sum)
    (sent,) = call(functools.partial(half_sums, 1), [half], *operands, smem=(0,), mib=SUMS)
    got = crossed(sent, "gz", 1)
    sent, xs = lax.optimization_barrier((sent, xs))
    back_t, back_g, kept = call(
        back_body,
        [lists, lists, ((ROWS, WIDE), BF)],
        xs, gos, mixed, dn, window_rows, gain, w_out,
        scratch=[pltpu.VMEM((SLOTS, WIDE), BF)],
        mib=BACK,
    )
    ways, places = (FIRST[::-1], SECOND[::-1]), starts()
    down = step([[back_t], [back_g]], places, ways, 0, -1)
    (own,) = call(functools.partial(half_sums, 0), [half], *operands, smem=(0,), mib=SUMS)

    (paired,) = call(sum1_body, [half], own, got)
    paired, down = lax.optimization_barrier((paired, down))
    down = step(down, places, ways, 1, -1)
    spread = lax.all_to_all(paired, ("gx", "gy"), split_axis=0, concat_axis=0, tiled=True)
    parts = call(sum2_body, [((4, COLS), BF)] * 4, spread.reshape(32, 16, COLS))
    parts, down = lax.optimization_barrier((parts, down))
    down = step(down, places, ways, 2, -1)
    last = [parts[0]] + [crossed(parts[i], "gz", 2 * i) for i in range(1, 4)]
    grad_qkv, grad_proj, gain_rows = call(
        sum3_body, [((3, 3 * D), F32), ((3, D), F32), ((3, 128), F32)], *last
    )

    block_out, grad_tokens = call(
        join_body,
        [((ROWS, D), BF), ((ROWS, D), BF)],
        kept, down[0][1:], down[1][1:], send_rows,
        scratch=[
            pltpu.VMEM((ROWS, WIDE), BF),
            pltpu.VMEM((224, WIDE), BF),
            pltpu.SemaphoreType.DMA((3, 8)),
        ],
        outside=range(7),
    )
    return (block_out, grad_tokens, gain_rows[:, 0], grad_qkv, grad_proj)


def solution(mesh):
    spread = P(AXES, None)
    in_specs = (spread, P(), P(), P(), P(AXES, None, None), spread, spread)
    out_specs = (spread, spread, P(AXES), spread, spread)
    return jax.shard_map(
        on_device, mesh=mesh, in_specs=in_specs, out_specs=out_specs, check_vma=False
    )
```

```python
import functools

import jax
import jax.numpy as jnp
from jax import lax
from jax.experimental import pallas as pl
from jax.experimental.pallas import tpu as pltpu
from jax.sharding import PartitionSpec as P

D = 768
WCAP = 128
SLOTS = 512
ROWS = 256
WIDE = 2 * D
HALF = 512
MAIN, BACK, SUMS, SMALL = 18, 16, 12, 6
COLS = 3 * D + 128
AXES = ("gx", "gy", "gz")
UP = (("gx", "gy", "gz"), ("gz", "gx", "gy"))
DOWN = (("gz", "gy", "gx"), ("gx", "gz", "gy"))
EPSILON = 1e-06
BIG_NEGATIVE = -1e30
BF = jnp.bfloat16
F32 = jnp.float32
NT = (((1,), (1,)), ((), ()))
TN = (((0,), (0,)), ((), ()))
VMEM = pl.BlockSpec(memory_space=pltpu.VMEM)
SMEM = pl.BlockSpec(memory_space=pltpu.SMEM)
ANY = pl.BlockSpec(memory_space=pl.ANY)


def dot(a, b):
    return jnp.dot(a, b, preferred_element_type=F32)


def iota(shape, dim):
    return lax.broadcasted_iota(jnp.int32, shape, dim)


def column(row):
    n = row.shape[1]
    spread = jnp.broadcast_to(row.astype(F32), (n, n))
    return jnp.sum(jnp.where(iota((n, n), 0) == iota((n, n), 1), spread, 0.0), axis=1, keepdims=True)


def one_hot(condition):
    return jnp.where(condition, 1.0, 0.0).astype(BF)


def passed_along(value, axis, steps):
    count = lax.axis_size(axis)
    initial, last = (max(0, -steps), min(count, count - steps))
    return lax.ppermute(value, axis, [(source, source + steps) for source in range(initial, last)])


def bit(k, axis):
    return k // (4, 2, 1)[AXES.index(axis)] % 2


def stage(arrays, place, axis, steps):
    moving = [k for k in range(1, 8) if bit(k, axis)]
    blocks = [lax.slice_in_dim(arrays[place[k][0]], place[k][1], place[k][1] + 1) for k in moving]
    for i, k in enumerate(moving):
        place[k] = (len(arrays), i)
    return [*arrays, passed_along(jnp.concatenate(blocks), axis, steps)]


def starts():
    return [{k: (0, k - 1) for k in range(1, 8)} for _ in range(2)]


def step(pair, places, ways, number, steps):
    return [
        stage(arrays, place, way[number], steps) for arrays, place, way in zip(pair, places, ways)
    ]


def arrival(axes):
    for k in range(1, 8):
        stage = max(s for s, axis in enumerate(axes) if bit(k, axis))
        moving = [m for m in range(1, 8) if bit(m, axes[stage])]
        yield stage, moving.index(k)


def crossed(value, axis, mask):
    count = lax.axis_size(axis)
    return lax.ppermute(value, axis, [(source, source ^ mask) for source in range(count)])


def named(send_ref):
    rows = [one_hot(iota((32, ROWS), 1).astype(F32) == column(send_ref[0, k : k + 1, :])) for k in range(7)]
    return jnp.concatenate(rows, axis=0)


def fetches(t_refs, g_refs, axes, to_ref, start, sems):
    copies = []
    for part, (refs, way) in enumerate(((t_refs, axes[0]), (g_refs, axes[1]))):
        for k, (stage, i) in enumerate(arrival(way)):
            at = to_ref.at[pl.ds(start + 32 * k, 32), pl.ds(part * D, D)]
            copies.append(pltpu.make_async_copy(refs[stage].at[i], at, sems.at[part, k]))
    return copies


def pack_body(tok_ref, go_ref, send_ref, *outs):
    chosen = named(send_ref)
    for part, ref in enumerate((tok_ref, go_ref)):
        outs[part][...] = dot(chosen, ref[...]).astype(BF).reshape(7, 32, D)


def normalised(x):
    centred = x - jnp.mean(x, axis=-1, keepdims=True)
    inv_std = lax.rsqrt(jnp.mean(centred * centred, axis=-1, keepdims=True) + EPSILON)
    return centred * inv_std, inv_std


def first_row(gz, core, block):
    gx, gy, z_hi = block // 16, block % 16 // 4, block % 4
    return ((gx * 4 + gy) * 8 + ((z_hi * 2 + core) ^ gz)) * 3


def half_place(gz, core):
    j = iota((HALF, 1), 0)
    row = jnp.where(j % 4 < 3, first_row(gz, core, j // 4) + j % 4, -1)
    return iota((HALF, D), 1) == row


def half_sums(core, me_ref, normed_ref, mixed_ref, gos_ref, dpacked_ref, gain_ref, out_ref):
    gz = me_ref[0]
    place = half_place(gz, core)
    turned = lax.dot_general(one_hot(place), normed_ref[...], NT, preferred_element_type=F32).astype(BF)
    i = iota((384, 1), 0)
    picks = one_hot(iota((384, D), 1) == first_row(gz, core, i % 128) + i // 128)
    picks = lax.dot_general(picks, mixed_ref[...], NT, preferred_element_type=F32).astype(BF)
    proj = dot(picks, gos_ref[...]).astype(BF)
    j = iota((HALF, 1), 0)
    widen = one_hot(iota((HALF, 128), 1) == jnp.where(j % 4 == 3, j // 4, -1))
    for g in range(3):
        at = slice(g * D, (g + 1) * D)
        total = dot(turned, dpacked_ref[:, at]) + dot(widen, proj[g * 128 : (g + 1) * 128])
        out_ref[:, at] = total.astype(BF)
    gains = jnp.sum(jnp.where(place, gain_ref[...], 0.0), axis=1, keepdims=True)
    out_ref[:, 3 * D :] = jnp.broadcast_to(gains, (HALF, 128)).astype(BF)


def main_body(
    tok_ref, go_ref, t_refs, g_refs, win_ref, gain_ref, wqkv_ref, wout_ref,
    xs_ref, gos_ref, normed_ref, mixed_ref, dpacked_ref, dn_ref, gain_sum_ref,
    rows_ref, packed_ref, delta_ref, held_ref, sems,
):
    copies = fetches(t_refs, g_refs, UP, rows_ref, ROWS, sems)
    own = rows_ref.at[pl.ds(0, ROWS), :]
    copies.append(pltpu.make_async_copy(tok_ref, own.at[:, pl.ds(0, D)], sems.at[0, 7]))
    copies.append(pltpu.make_async_copy(go_ref, own.at[:, pl.ds(D, D)], sems.at[1, 7]))
    weights_copy = pltpu.make_async_copy(wout_ref, held_ref, sems.at[2, 0])
    for copy in copies:
        copy.start()
    weights_copy.start()
    rows_ref[480:, :] = jnp.zeros((32, WIDE), BF)
    gain = gain_ref[...]
    for copy in copies:
        copy.wait()

    def gather_window(w, carry):
        at = pl.ds(pl.multiple_of(w * WCAP, WCAP), WCAP)
        picks = one_hot(iota((WCAP, SLOTS), 1).astype(F32) == column(win_ref[:, at]))
        taken = dot(picks, rows_ref[...])
        x = taken[:, :D]
        xs_ref[at, :] = x.astype(BF)
        gos_ref[at, :] = taken[:, D:].astype(BF)
        unit, _ = normalised(x)
        normed_ref[at, :] = (unit * gain).astype(BF)
        return carry

    lax.fori_loop(0, SLOTS // WCAP, gather_window, 0)

    def project(c, carry):
        at = pl.ds(pl.multiple_of(c * D, D), D)
        packed_ref[:, at] = dot(normed_ref[...], wqkv_ref[:, at]).astype(BF)
        return carry

    lax.fori_loop(0, 3, project, 0)
    weights_copy.wait()
    delta_ref[...] = lax.dot_general(
        gos_ref[...], held_ref[...], NT, preferred_element_type=F32
    ).astype(BF)

    low = iota((WCAP, 128), 1) < 64
    zero = jnp.zeros((), BF)

    def both(value):
        return jnp.concatenate([jnp.where(low, value, zero), jnp.where(low, zero, value)], axis=0)

    def attend(w, carry):
        at = pl.ds(pl.multiple_of(w * WCAP, WCAP), WCAP)
        filled = jnp.broadcast_to(column(win_ref[:, at]) >= 0, (WCAP, WCAP))[None]
        for p in range(6):
            q_at = pl.ds(p * 128, 128)
            k_at = pl.ds(D + p * 128, 128)
            v_at = pl.ds(2 * D + p * 128, 128)
            q = packed_ref[at, q_at]
            k_both = both(packed_ref[at, k_at])
            v_both = both(packed_ref[at, v_at])
            d = delta_ref[at, q_at]
            scores = lax.dot_general(k_both, q, NT, preferred_element_type=F32) * 0.125
            scores = jnp.where(filled, scores.reshape(2, WCAP, WCAP), BIG_NEGATIVE)
            expo = jnp.exp(scores - jnp.max(scores, axis=1, keepdims=True))
            probs = expo * (1.0 / jnp.sum(expo, axis=1, keepdims=True))
            weights = probs.astype(BF)
            mixed = lax.dot_general(
                weights.reshape(2 * WCAP, WCAP), v_both, TN, preferred_element_type=F32
            )
            mixed_ref[at, q_at] = mixed.astype(BF)
            dweights = lax.dot_general(v_both, d, NT, preferred_element_type=F32)
            dweights = dweights.reshape(2, WCAP, WCAP)
            inner = jnp.sum(dweights * probs, axis=1, keepdims=True)
            dscaled = (probs * (dweights - inner) * 0.125).astype(BF)
            dq = lax.dot_general(
                dscaled.reshape(2 * WCAP, WCAP), k_both, TN, preferred_element_type=F32
            )
            dpacked_ref[at, q_at] = dq.astype(BF)
            beside = jnp.concatenate([dscaled[0], dscaled[1]], axis=1)
            dpacked_ref[at, k_at] = dot(beside, both(q)).astype(BF)
            beside = jnp.concatenate([weights[0], weights[1]], axis=1)
            dpacked_ref[at, v_at] = dot(beside, both(d)).astype(BF)
        return carry

    lax.fori_loop(0, SLOTS // WCAP, attend, 0)
    dnormed = lax.dot_general(
        dpacked_ref[...], wqkv_ref[...], NT, preferred_element_type=F32
    ).astype(BF)
    dn_ref[...] = dnormed
    unit, _ = normalised(xs_ref[...].astype(F32))
    gain_sum_ref[...] = jnp.sum(dnormed.astype(F32) * unit, axis=0, keepdims=True)


def back_body(
    xs_ref, gos_ref, mixed_ref, dn_ref, win_ref, gain_ref, wout_ref, t_ref, g_ref, kept_ref, cat_ref,
):
    gain = gain_ref[...]
    projected = dot(mixed_ref[...], wout_ref[...])
    cat_ref[:, :D] = (xs_ref[...].astype(F32) + projected).astype(BF)
    for w in range(4):
        at = slice(w * WCAP, (w + 1) * WCAP)
        unit, inv_std = normalised(xs_ref[at, :].astype(F32))
        dnormed = dn_ref[at, :].astype(F32)
        dunit = dnormed * gain
        dcentre = inv_std * (
            dunit
            - jnp.mean(dunit, axis=-1, keepdims=True)
            - unit * jnp.mean(dunit * unit, axis=-1, keepdims=True)
        )
        cat_ref[at, D:] = (gos_ref[at, :].astype(F32) + dcentre).astype(BF)
    back = one_hot(iota((480, SLOTS), 0) == win_ref[...])
    kept_ref[...] = dot(back[:ROWS], cat_ref[...]).astype(BF)
    sent = dot(back[ROWS:], cat_ref[...]).astype(BF).reshape(7, 32, WIDE)
    t_ref[...] = sent[:, :, :D]
    g_ref[...] = sent[:, :, D:]


def join_body(kept_ref, t_refs, g_refs, send_ref, out_ref, grad_ref, own_ref, rows_ref, sems):
    copies = fetches(t_refs, g_refs, DOWN, rows_ref, 0, sems)
    copies.append(pltpu.make_async_copy(kept_ref, own_ref, sems.at[2, 0]))
    for copy in copies:
        copy.start()
    chosen = named(send_ref)
    for copy in copies:
        copy.wait()
    for part, out in enumerate((out_ref, grad_ref)):
        at = slice(part * D, (part + 1) * D)
        back = lax.dot_general(chosen, rows_ref[:, at], TN, preferred_element_type=F32)
        out[...] = (own_ref[:, at].astype(F32) + back).astype(BF)


def sum1_body(own_ref, got_ref, out_ref):
    out_ref[...] = (own_ref[...].astype(F32) + got_ref[...].astype(F32)).astype(BF)


def sum2_body(me_ref, got_ref, out_ref):
    total = jnp.sum(got_ref[...].astype(F32), axis=0)
    for i in range(4):
        rows = jnp.concatenate([total[4 * i : 4 * (i + 1)], jnp.zeros((4, COLS), F32)])
        out_ref[(me_ref[0] // 2) ^ i] = rows.astype(BF)


def sum3_body(got_ref, qkv_ref, out_ref, gain_ref):
    total = jnp.sum(got_ref[...].astype(F32), axis=0)
    qkv_ref[...] = total[:3, : 3 * D]
    for g in range(3):
        out_ref[g : g + 1, :] = total[3:4, g * D : (g + 1) * D]
    gain_ref[...] = total[:3, 3 * D :]


def call(body, shapes, *args, scratch=(), smem=(), outside=(), mib=SMALL):
    tree = jax.tree.structure(args)
    count = tree.num_leaves

    def flat(*refs):
        body(*jax.tree.unflatten(tree, refs[:count]), *refs[count:])

    return pl.pallas_call(
        flat,
        out_shape=[jax.ShapeDtypeStruct(shape, dtype) for shape, dtype in shapes],
        in_specs=[ANY if i in outside else SMEM if i in smem else VMEM for i in range(count)],
        out_specs=[VMEM] * len(shapes),
        scratch_shapes=list(scratch),
        compiler_params=pltpu.CompilerParams(vmem_limit_bytes=mib * 1024 * 1024),
    )(*jax.tree.leaves(args))


def on_device(tokens, norm_gain, w_qkv, w_out, send_rows, window_rows, grad_out):
    gain = norm_gain.reshape(1, D)
    me = lax.axis_index("gz").astype(jnp.int32).reshape(1)
    me, tokens, grad_out = lax.optimization_barrier((me, tokens, grad_out))
    lists = ((7, 32, D), BF)
    blocks = call(pack_body, [lists, lists], tokens, grad_out, send_rows)
    up = [[blocks[0]], [blocks[1]]]
    places = starts()
    for number in range(3):
        up = step(up, places, UP, number, 1)
    arrived_t, arrived_g = up[0][1:], up[1][1:]

    slot, wide, half = ((SLOTS, D), BF), ((SLOTS, 3 * D), BF), ((HALF, COLS), BF)
    xs, gos, normed, mixed, dpacked, dn, gain_sum = call(
        main_body,
        [slot, slot, slot, slot, wide, slot, ((1, D), F32)],
        tokens, grad_out, arrived_t, arrived_g, window_rows, gain, w_qkv, w_out,
        scratch=[
            pltpu.VMEM((SLOTS, WIDE), BF),
            pltpu.VMEM(*wide),
            pltpu.VMEM(*slot),
            pltpu.VMEM((D, D), BF),
            pltpu.SemaphoreType.DMA((3, 8)),
        ],
        outside=(0, 1, 2, 3, 4, 5, 6, 7, 11),
        mib=MAIN,
    )
    operands = (me, normed, mixed, gos, dpacked, gain_sum)
    (sent,) = call(functools.partial(half_sums, 1), [half], *operands, smem=(0,), mib=SUMS)
    got = crossed(sent, "gz", 1)
    sent, xs = lax.optimization_barrier((sent, xs))
    back_t, back_g, kept = call(
        back_body,
        [lists, lists, ((ROWS, WIDE), BF)],
        xs, gos, mixed, dn, window_rows, gain, w_out,
        scratch=[pltpu.VMEM((SLOTS, WIDE), BF)],
        mib=BACK,
    )
    places = starts()
    down = step([[back_t], [back_g]], places, DOWN, 0, -1)
    (own,) = call(functools.partial(half_sums, 0), [half], *operands, smem=(0,), mib=SUMS)

    (paired,) = call(sum1_body, [half], own, got)
    paired, down = lax.optimization_barrier((paired, down))
    down = step(down, places, DOWN, 1, -1)
    spread = lax.all_to_all(paired, ("gx", "gy"), split_axis=0, concat_axis=0, tiled=True)
    (part,) = call(sum2_body, [((4, 8, COLS), BF)], me, spread.reshape(32, 16, COLS), smem=(0,))
    part, down = lax.optimization_barrier((part, down))
    down = step(down, places, DOWN, 2, -1)
    groups = [[2 * i + core for i in range(4)] for core in range(2)]
    last = lax.all_to_all(
        part, "gz", split_axis=0, concat_axis=0, tiled=True, axis_index_groups=groups
    )
    grad_qkv, grad_proj, gain_rows = call(
        sum3_body, [((3, 3 * D), F32), ((3, D), F32), ((3, 128), F32)], last
    )

    block_out, grad_tokens = call(
        join_body,
        [((ROWS, D), BF), ((ROWS, D), BF)],
        kept, down[0][1:], down[1][1:], send_rows,
        scratch=[
            pltpu.VMEM((ROWS, WIDE), BF),
            pltpu.VMEM((224, WIDE), BF),
            pltpu.SemaphoreType.DMA((3, 8)),
        ],
        outside=range(7),
    )
    return (block_out, grad_tokens, gain_rows[:, 0], grad_qkv, grad_proj)


def solution(mesh):
    spread = P(AXES, None)
    in_specs = (spread, P(), P(), P(), P(AXES, None, None), spread, spread)
    out_specs = (spread, spread, P(AXES), spread, spread)
    return jax.shard_map(
        on_device, mesh=mesh, in_specs=in_specs, out_specs=out_specs, check_vma=False
    )
```

```python
import functools

import jax
import jax.numpy as jnp
from jax import lax
from jax.experimental import pallas as pl
from jax.experimental.pallas import tpu as pltpu
from jax.sharding import PartitionSpec as P

D = 768
WCAP = 128
SLOTS = 512
ROWS = 256
WIDE = 2 * D
HALF = 512
MAIN, BACK, SUMS, SMALL = 18, 16, 12, 6
COLS = 3 * D + 128
AXES = ("gx", "gy", "gz")
UP = (("gx", "gy", "gz"), ("gz", "gx", "gy"))
DOWN = (("gz", "gy", "gx"), ("gx", "gz", "gy"))
EPSILON = 1e-06
BIG_NEGATIVE = -1e30
BF = jnp.bfloat16
F32 = jnp.float32
NT = (((1,), (1,)), ((), ()))
TN = (((0,), (0,)), ((), ()))
VMEM = pl.BlockSpec(memory_space=pltpu.VMEM)
SMEM = pl.BlockSpec(memory_space=pltpu.SMEM)
ANY = pl.BlockSpec(memory_space=pl.ANY)


def dot(a, b):
    return jnp.dot(a, b, preferred_element_type=F32)


def iota(shape, dim):
    return lax.broadcasted_iota(jnp.int32, shape, dim)


def column(row):
    n = row.shape[1]
    spread = jnp.broadcast_to(row.astype(F32), (n, n))
    return jnp.sum(jnp.where(iota((n, n), 0) == iota((n, n), 1), spread, 0.0), axis=1, keepdims=True)


def one_hot(condition):
    return jnp.where(condition, 1.0, 0.0).astype(BF)


def passed_along(value, axis, steps):
    count = lax.axis_size(axis)
    initial, last = (max(0, -steps), min(count, count - steps))
    return lax.ppermute(value, axis, [(source, source + steps) for source in range(initial, last)])


def bit(k, axis):
    return k // (4, 2, 1)[AXES.index(axis)] % 2


def stage(arrays, place, axis, steps):
    moving = [k for k in range(1, 8) if bit(k, axis)]
    blocks = [lax.slice_in_dim(arrays[place[k][0]], place[k][1], place[k][1] + 1) for k in moving]
    for i, k in enumerate(moving):
        place[k] = (len(arrays), i)
    return [*arrays, passed_along(jnp.concatenate(blocks), axis, steps)]


def starts():
    return [{k: (0, k - 1) for k in range(1, 8)} for _ in range(2)]


def step(pair, places, ways, number, steps):
    return [
        stage(arrays, place, way[number], steps) for arrays, place, way in zip(pair, places, ways)
    ]


def arrival(axes):
    for k in range(1, 8):
        stage = max(s for s, axis in enumerate(axes) if bit(k, axis))
        moving = [m for m in range(1, 8) if bit(m, axes[stage])]
        yield stage, moving.index(k)


def crossed(value, axis, mask):
    count = lax.axis_size(axis)
    return lax.ppermute(value, axis, [(source, source ^ mask) for source in range(count)])


def named(send_ref):
    rows = [one_hot(iota((32, ROWS), 1).astype(F32) == column(send_ref[0, k : k + 1, :])) for k in range(7)]
    return jnp.concatenate(rows, axis=0)


def fetches(t_refs, g_refs, axes, to_ref, start, sems):
    copies = []
    for part, (refs, way) in enumerate(((t_refs, axes[0]), (g_refs, axes[1]))):
        for k, (stage, i) in enumerate(arrival(way)):
            at = to_ref.at[pl.ds(start + 32 * k, 32), pl.ds(part * D, D)]
            copies.append(pltpu.make_async_copy(refs[stage].at[i], at, sems.at[part, k]))
    return copies


def pack_body(tok_ref, go_ref, send_ref, *outs):
    chosen = named(send_ref)
    for part, ref in enumerate((tok_ref, go_ref)):
        outs[part][...] = dot(chosen, ref[...]).astype(BF).reshape(7, 32, D)


def normalised(x):
    centred = x - jnp.mean(x, axis=-1, keepdims=True)
    inv_std = lax.rsqrt(jnp.mean(centred * centred, axis=-1, keepdims=True) + EPSILON)
    return centred * inv_std, inv_std


def first_row(gz, core, block):
    gx, gy, z_hi = block // 16, block % 16 // 4, block % 4
    return ((gx * 4 + gy) * 8 + ((z_hi * 2 + core) ^ gz)) * 3


def half_place(gz, core):
    j = iota((HALF, 1), 0)
    row = jnp.where(j % 4 < 3, first_row(gz, core, j // 4) + j % 4, -1)
    return iota((HALF, D), 1) == row


def with_other(total, at, rest):
    return total + rest[0][:, at].astype(F32) if len(rest) == 2 else total


def half_sums(core, me_ref, normed_ref, mixed_ref, gos_ref, dpacked_ref, gain_ref, *rest):
    out_ref = rest[-1]
    gz = me_ref[0]
    place = half_place(gz, core)
    turned = lax.dot_general(one_hot(place), normed_ref[...], NT, preferred_element_type=F32).astype(BF)
    i = iota((384, 1), 0)
    picks = one_hot(iota((384, D), 1) == first_row(gz, core, i % 128) + i // 128)
    picks = lax.dot_general(picks, mixed_ref[...], NT, preferred_element_type=F32).astype(BF)
    proj = dot(picks, gos_ref[...]).astype(BF)
    j = iota((HALF, 1), 0)
    widen = one_hot(iota((HALF, 128), 1) == jnp.where(j % 4 == 3, j // 4, -1))
    for g in range(3):
        at = slice(g * D, (g + 1) * D)
        total = dot(turned, dpacked_ref[:, at]) + dot(widen, proj[g * 128 : (g + 1) * 128])
        out_ref[:, at] = with_other(total, at, rest).astype(BF)
    gains = jnp.sum(jnp.where(place, gain_ref[...], 0.0), axis=1, keepdims=True)
    gains = jnp.broadcast_to(gains, (HALF, 128))
    at = slice(3 * D, COLS)
    out_ref[:, at] = with_other(gains, at, rest).astype(BF)


def main_body(
    tok_ref, go_ref, t_refs, g_refs, win_ref, gain_ref, wqkv_ref, wout_ref,
    xs_ref, gos_ref, normed_ref, mixed_ref, dpacked_ref, dn_ref, gain_sum_ref,
    rows_ref, packed_ref, delta_ref, held_ref, sems,
):
    copies = fetches(t_refs, g_refs, UP, rows_ref, ROWS, sems)
    own = rows_ref.at[pl.ds(0, ROWS), :]
    copies.append(pltpu.make_async_copy(tok_ref, own.at[:, pl.ds(0, D)], sems.at[0, 7]))
    copies.append(pltpu.make_async_copy(go_ref, own.at[:, pl.ds(D, D)], sems.at[1, 7]))
    weights_copy = pltpu.make_async_copy(wout_ref, held_ref, sems.at[2, 0])
    for copy in copies:
        copy.start()
    weights_copy.start()
    rows_ref[480:, :] = jnp.zeros((32, WIDE), BF)
    gain = gain_ref[...]
    for copy in copies:
        copy.wait()

    def gather_window(w, carry):
        at = pl.ds(pl.multiple_of(w * WCAP, WCAP), WCAP)
        picks = one_hot(iota((WCAP, SLOTS), 1).astype(F32) == column(win_ref[:, at]))
        taken = dot(picks, rows_ref[...])
        x = taken[:, :D]
        xs_ref[at, :] = x.astype(BF)
        gos_ref[at, :] = taken[:, D:].astype(BF)
        unit, _ = normalised(x)
        normed_ref[at, :] = (unit * gain).astype(BF)
        return carry

    lax.fori_loop(0, SLOTS // WCAP, gather_window, 0, unroll=True)

    def project(c, carry):
        at = pl.ds(pl.multiple_of(c * D, D), D)
        packed_ref[:, at] = dot(normed_ref[...], wqkv_ref[:, at]).astype(BF)
        return carry

    lax.fori_loop(0, 3, project, 0)
    weights_copy.wait()
    delta_ref[...] = lax.dot_general(
        gos_ref[...], held_ref[...], NT, preferred_element_type=F32
    ).astype(BF)

    low = iota((WCAP, 128), 1) < 64
    zero = jnp.zeros((), BF)

    def both(value):
        return jnp.concatenate([jnp.where(low, value, zero), jnp.where(low, zero, value)], axis=0)

    def attend(w, carry):
        at = pl.ds(pl.multiple_of(w * WCAP, WCAP), WCAP)
        filled = jnp.broadcast_to(column(win_ref[:, at]) >= 0, (WCAP, WCAP))[None]
        for p in range(6):
            q_at = pl.ds(p * 128, 128)
            k_at = pl.ds(D + p * 128, 128)
            v_at = pl.ds(2 * D + p * 128, 128)
            q = packed_ref[at, q_at]
            k_both = both(packed_ref[at, k_at])
            v_both = both(packed_ref[at, v_at])
            d = delta_ref[at, q_at]
            scaled = q * jnp.asarray(0.125, BF)
            scores = lax.dot_general(k_both, scaled, NT, preferred_element_type=F32)
            scores = jnp.where(filled, scores.reshape(2, WCAP, WCAP), BIG_NEGATIVE)
            expo = jnp.exp(scores - jnp.max(scores, axis=1, keepdims=True))
            probs = expo * (1.0 / jnp.sum(expo, axis=1, keepdims=True))
            weights = probs.astype(BF)
            mixed = lax.dot_general(
                weights.reshape(2 * WCAP, WCAP), v_both, TN, preferred_element_type=F32
            )
            mixed_ref[at, q_at] = mixed.astype(BF)
            dweights = lax.dot_general(v_both, d, NT, preferred_element_type=F32)
            dweights = dweights.reshape(2, WCAP, WCAP)
            inner = jnp.sum(dweights * probs, axis=1, keepdims=True)
            dscaled = (probs * (dweights - inner) * 0.125).astype(BF)
            dq = lax.dot_general(
                dscaled.reshape(2 * WCAP, WCAP), k_both, TN, preferred_element_type=F32
            )
            dpacked_ref[at, q_at] = dq.astype(BF)
            beside = jnp.concatenate([dscaled[0], dscaled[1]], axis=1)
            dpacked_ref[at, k_at] = dot(beside, both(q)).astype(BF)
            beside = jnp.concatenate([weights[0], weights[1]], axis=1)
            dpacked_ref[at, v_at] = dot(beside, both(d)).astype(BF)
        return carry

    lax.fori_loop(0, SLOTS // WCAP, attend, 0, unroll=True)
    dnormed = lax.dot_general(
        dpacked_ref[...], wqkv_ref[...], NT, preferred_element_type=F32
    ).astype(BF)
    dn_ref[...] = dnormed
    unit, _ = normalised(xs_ref[...].astype(F32))
    gain_sum_ref[...] = jnp.sum(dnormed.astype(F32) * unit, axis=0, keepdims=True)


def back_body(
    xs_ref, gos_ref, mixed_ref, dn_ref, win_ref, gain_ref, wout_ref, t_ref, g_ref, kept_ref, cat_ref,
):
    gain = gain_ref[...]
    projected = dot(mixed_ref[...], wout_ref[...])
    cat_ref[:, :D] = (xs_ref[...].astype(F32) + projected).astype(BF)
    for w in range(4):
        at = slice(w * WCAP, (w + 1) * WCAP)
        unit, inv_std = normalised(xs_ref[at, :].astype(F32))
        dnormed = dn_ref[at, :].astype(F32)
        dunit = dnormed * gain
        dcentre = inv_std * (
            dunit
            - jnp.mean(dunit, axis=-1, keepdims=True)
            - unit * jnp.mean(dunit * unit, axis=-1, keepdims=True)
        )
        cat_ref[at, D:] = (gos_ref[at, :].astype(F32) + dcentre).astype(BF)
    back = one_hot(iota((480, SLOTS), 0) == win_ref[...])
    kept_ref[...] = dot(back[:ROWS], cat_ref[...]).astype(BF)
    sent = dot(back[ROWS:], cat_ref[...]).astype(BF).reshape(7, 32, WIDE)
    t_ref[...] = sent[:, :, :D]
    g_ref[...] = sent[:, :, D:]


def join_body(kept_ref, t_refs, g_refs, send_ref, out_ref, grad_ref, own_ref, rows_ref, sems):
    copies = fetches(t_refs, g_refs, DOWN, rows_ref, 0, sems)
    copies.append(pltpu.make_async_copy(kept_ref, own_ref, sems.at[2, 0]))
    for copy in copies:
        copy.start()
    chosen = named(send_ref)
    for copy in copies:
        copy.wait()
    for part, out in enumerate((out_ref, grad_ref)):
        at = slice(part * D, (part + 1) * D)
        back = lax.dot_general(chosen, rows_ref[:, at], TN, preferred_element_type=F32)
        out[...] = (own_ref[:, at].astype(F32) + back).astype(BF)


def sum2_body(me_ref, got_ref, out_ref):
    total = jnp.sum(got_ref[...].astype(F32), axis=0)
    for i in range(4):
        rows = jnp.concatenate([total[4 * i : 4 * (i + 1)], jnp.zeros((4, COLS), F32)])
        out_ref[(me_ref[0] // 2) ^ i] = rows.astype(BF)


def sum3_body(got_ref, qkv_ref, out_ref, gain_ref):
    total = jnp.sum(got_ref[...].astype(F32), axis=0)
    qkv_ref[...] = total[:3, : 3 * D]
    for g in range(3):
        out_ref[g : g + 1, :] = total[3:4, g * D : (g + 1) * D]
    gain_ref[...] = total[:3, 3 * D :]


def call(body, shapes, *args, scratch=(), smem=(), outside=(), mib=SMALL):
    tree = jax.tree.structure(args)
    count = tree.num_leaves

    def flat(*refs):
        body(*jax.tree.unflatten(tree, refs[:count]), *refs[count:])

    return pl.pallas_call(
        flat,
        out_shape=[jax.ShapeDtypeStruct(shape, dtype) for shape, dtype in shapes],
        in_specs=[ANY if i in outside else SMEM if i in smem else VMEM for i in range(count)],
        out_specs=[VMEM] * len(shapes),
        scratch_shapes=list(scratch),
        compiler_params=pltpu.CompilerParams(vmem_limit_bytes=mib * 1024 * 1024),
    )(*jax.tree.leaves(args))


def on_device(tokens, norm_gain, w_qkv, w_out, send_rows, window_rows, grad_out):
    gain = norm_gain.reshape(1, D)
    me = lax.axis_index("gz").astype(jnp.int32).reshape(1)
    me, tokens, grad_out = lax.optimization_barrier((me, tokens, grad_out))
    lists = ((7, 32, D), BF)
    blocks = call(pack_body, [lists, lists], tokens, grad_out, send_rows)
    up = [[blocks[0]], [blocks[1]]]
    places = starts()
    for number in range(3):
        up = step(up, places, UP, number, 1)
    arrived_t, arrived_g = up[0][1:], up[1][1:]

    slot, wide, half = ((SLOTS, D), BF), ((SLOTS, 3 * D), BF), ((HALF, COLS), BF)
    xs, gos, normed, mixed, dpacked, dn, gain_sum = call(
        main_body,
        [slot, slot, slot, slot, wide, slot, ((1, D), F32)],
        tokens, grad_out, arrived_t, arrived_g, window_rows, gain, w_qkv, w_out,
        scratch=[
            pltpu.VMEM((SLOTS, WIDE), BF),
            pltpu.VMEM(*wide),
            pltpu.VMEM(*slot),
            pltpu.VMEM((D, D), BF),
            pltpu.SemaphoreType.DMA((3, 8)),
        ],
        outside=(0, 1, 2, 3, 4, 5, 6, 7, 11),
        mib=MAIN,
    )
    operands = (me, normed, mixed, gos, dpacked, gain_sum)
    (sent,) = call(functools.partial(half_sums, 1), [half], *operands, smem=(0,), mib=SUMS)
    got = crossed(sent, "gz", 1)
    sent, xs = lax.optimization_barrier((sent, xs))
    back_t, back_g, kept = call(
        back_body,
        [lists, lists, ((ROWS, WIDE), BF)],
        xs, gos, mixed, dn, window_rows, gain, w_out,
        scratch=[pltpu.VMEM((SLOTS, WIDE), BF)],
        mib=BACK,
    )
    places = starts()
    down = step([[back_t], [back_g]], places, DOWN, 0, -1)
    (paired,) = call(functools.partial(half_sums, 0), [half], *operands, got, smem=(0,), mib=SUMS)
    paired, down = lax.optimization_barrier((paired, down))
    down = step(down, places, DOWN, 1, -1)
    spread = lax.all_to_all(paired, ("gx", "gy"), split_axis=0, concat_axis=0, tiled=True)
    (part,) = call(sum2_body, [((4, 8, COLS), BF)], me, spread.reshape(32, 16, COLS), smem=(0,))
    part, down = lax.optimization_barrier((part, down))
    down = step(down, places, DOWN, 2, -1)
    groups = [[2 * i + core for i in range(4)] for core in range(2)]
    last = lax.all_to_all(
        part, "gz", split_axis=0, concat_axis=0, tiled=True, axis_index_groups=groups
    )
    grad_qkv, grad_proj, gain_rows = call(
        sum3_body, [((3, 3 * D), F32), ((3, D), F32), ((3, 128), F32)], last
    )

    block_out, grad_tokens = call(
        join_body,
        [((ROWS, D), BF), ((ROWS, D), BF)],
        kept, down[0][1:], down[1][1:], send_rows,
        scratch=[
            pltpu.VMEM((ROWS, WIDE), BF),
            pltpu.VMEM((224, WIDE), BF),
            pltpu.SemaphoreType.DMA((3, 8)),
        ],
        outside=range(7),
    )
    return (block_out, grad_tokens, gain_rows[:, 0], grad_qkv, grad_proj)


def solution(mesh):
    spread = P(AXES, None)
    in_specs = (spread, P(), P(), P(), P(AXES, None, None), spread, spread)
    out_specs = (spread, spread, P(AXES), spread, spread)
    return jax.shard_map(
        on_device, mesh=mesh, in_specs=in_specs, out_specs=out_specs, check_vma=False
    )
```

```python
import functools

import jax
import jax.numpy as jnp
from jax import lax
from jax.experimental import pallas as pl
from jax.experimental.pallas import tpu as pltpu
from jax.sharding import PartitionSpec as P

D = 768
WCAP = 128
SLOTS = 512
ROWS = 256
WIDE = 2 * D
HALF = 512
MAIN, BACK, SUMS, SMALL = 18, 16, 12, 6
COLS = 3 * D + 128
AXES = ("gx", "gy", "gz")
UP = (("gx", "gy", "gz"), ("gz", "gx", "gy"))
DOWN = (("gz", "gy", "gx"), ("gx", "gz", "gy"))
EPSILON = 1e-06
BIG_NEGATIVE = -1e30
BF = jnp.bfloat16
F32 = jnp.float32
NT = (((1,), (1,)), ((), ()))
TN = (((0,), (0,)), ((), ()))
VMEM = pl.BlockSpec(memory_space=pltpu.VMEM)
SMEM = pl.BlockSpec(memory_space=pltpu.SMEM)
ANY = pl.BlockSpec(memory_space=pl.ANY)


def dot(a, b):
    return jnp.dot(a, b, preferred_element_type=F32)


def iota(shape, dim):
    return lax.broadcasted_iota(jnp.int32, shape, dim)


def column(row):
    n = row.shape[1]
    spread = jnp.broadcast_to(row.astype(F32), (n, n))
    return jnp.sum(jnp.where(iota((n, n), 0) == iota((n, n), 1), spread, 0.0), axis=1, keepdims=True)


def one_hot(condition):
    return jnp.where(condition, 1.0, 0.0).astype(BF)


def passed_along(value, axis, steps):
    count = lax.axis_size(axis)
    initial, last = (max(0, -steps), min(count, count - steps))
    return lax.ppermute(value, axis, [(source, source + steps) for source in range(initial, last)])


def bit(k, axis):
    return k // (4, 2, 1)[AXES.index(axis)] % 2


def stage(arrays, place, axis, steps):
    moving = [k for k in range(1, 8) if bit(k, axis)]
    blocks = [lax.slice_in_dim(arrays[place[k][0]], place[k][1], place[k][1] + 1) for k in moving]
    for i, k in enumerate(moving):
        place[k] = (len(arrays), i)
    return [*arrays, passed_along(jnp.concatenate(blocks), axis, steps)]


def starts():
    return [{k: (0, k - 1) for k in range(1, 8)} for _ in range(2)]


def step(pair, places, ways, number, steps):
    return [
        stage(arrays, place, way[number], steps) for arrays, place, way in zip(pair, places, ways)
    ]


def arrival(axes):
    for k in range(1, 8):
        stage = max(s for s, axis in enumerate(axes) if bit(k, axis))
        moving = [m for m in range(1, 8) if bit(m, axes[stage])]
        yield stage, moving.index(k)


def crossed(value, axis, mask):
    count = lax.axis_size(axis)
    return lax.ppermute(value, axis, [(source, source ^ mask) for source in range(count)])


def named(send_ref):
    rows = [one_hot(iota((32, ROWS), 1).astype(F32) == column(send_ref[0, k : k + 1, :])) for k in range(7)]
    return jnp.concatenate(rows, axis=0)


def fetches(t_refs, g_refs, axes, to_ref, start, sems):
    copies = []
    for part, (refs, way) in enumerate(((t_refs, axes[0]), (g_refs, axes[1]))):
        for k, (stage, i) in enumerate(arrival(way)):
            at = to_ref.at[pl.ds(start + 32 * k, 32), pl.ds(part * D, D)]
            copies.append(pltpu.make_async_copy(refs[stage].at[i], at, sems.at[part, k]))
    return copies


def pack_body(tok_ref, go_ref, send_ref, *outs):
    chosen = named(send_ref)
    for part, ref in enumerate((tok_ref, go_ref)):
        outs[part][...] = dot(chosen, ref[...]).astype(BF).reshape(7, 32, D)


def normalised(x):
    centred = x - jnp.mean(x, axis=-1, keepdims=True)
    inv_std = lax.rsqrt(jnp.mean(centred * centred, axis=-1, keepdims=True) + EPSILON)
    return centred * inv_std, inv_std


def first_row(gz, core, block):
    gx, gy, z_hi = block // 16, block % 16 // 4, block % 4
    return ((gx * 4 + gy) * 8 + ((z_hi * 2 + core) ^ gz)) * 3


def half_place(gz, core):
    j = iota((HALF, 1), 0)
    row = jnp.where(j % 4 < 3, first_row(gz, core, j // 4) + j % 4, -1)
    return iota((HALF, D), 1) == row


def with_other(total, at, rest):
    return total + rest[0][:, at].astype(F32) if len(rest) == 2 else total


def half_sums(core, me_ref, normed_ref, mixed_ref, gos_ref, dpacked_ref, gain_ref, *rest):
    out_ref = rest[-1]
    gz = me_ref[0]
    place = half_place(gz, core)
    turned = lax.dot_general(one_hot(place), normed_ref[...], NT, preferred_element_type=F32).astype(BF)
    i = iota((384, 1), 0)
    picks = one_hot(iota((384, D), 1) == first_row(gz, core, i % 128) + i // 128)
    picks = lax.dot_general(picks, mixed_ref[...], NT, preferred_element_type=F32).astype(BF)
    proj = dot(picks, gos_ref[...]).astype(BF)
    j = iota((HALF, 1), 0)
    widen = one_hot(iota((HALF, 128), 1) == jnp.where(j % 4 == 3, j // 4, -1))
    for g in range(3):
        at = slice(g * D, (g + 1) * D)
        total = dot(turned, dpacked_ref[:, at]) + dot(widen, proj[g * 128 : (g + 1) * 128])
        out_ref[:, at] = with_other(total, at, rest).astype(BF)
    gains = jnp.sum(jnp.where(place, gain_ref[...], 0.0), axis=1, keepdims=True)
    gains = jnp.broadcast_to(gains, (HALF, 128))
    at = slice(3 * D, COLS)
    out_ref[:, at] = with_other(gains, at, rest).astype(BF)


def main_body(
    tok_ref, go_ref, t_refs, g_refs, win_ref, gain_ref, wqkv_ref, wout_ref,
    xs_ref, gos_ref, normed_ref, mixed_ref, dpacked_ref, dn_ref, gain_sum_ref,
    rows_ref, packed_ref, delta_ref, held_ref, sems,
):
    copies = fetches(t_refs, g_refs, UP, rows_ref, ROWS, sems)
    own = rows_ref.at[pl.ds(0, ROWS), :]
    copies.append(pltpu.make_async_copy(tok_ref, own.at[:, pl.ds(0, D)], sems.at[0, 7]))
    copies.append(pltpu.make_async_copy(go_ref, own.at[:, pl.ds(D, D)], sems.at[1, 7]))
    weights_copy = pltpu.make_async_copy(wout_ref, held_ref, sems.at[2, 0])
    for copy in copies:
        copy.start()
    weights_copy.start()
    rows_ref[480:, :] = jnp.zeros((32, WIDE), BF)
    gain = gain_ref[...]
    for copy in copies:
        copy.wait()

    def gather_window(w, carry):
        at = pl.ds(pl.multiple_of(w * WCAP, WCAP), WCAP)
        picks = one_hot(iota((WCAP, SLOTS), 1).astype(F32) == column(win_ref[:, at]))
        taken = dot(picks, rows_ref[...])
        x = taken[:, :D]
        xs_ref[at, :] = x.astype(BF)
        gos_ref[at, :] = taken[:, D:].astype(BF)
        unit, _ = normalised(x)
        normed_ref[at, :] = (unit * gain).astype(BF)
        return carry

    lax.fori_loop(0, SLOTS // WCAP, gather_window, 0, unroll=True)

    def project(c, carry):
        at = pl.ds(pl.multiple_of(c * D, D), D)
        packed_ref[:, at] = dot(normed_ref[...], wqkv_ref[:, at]).astype(BF)
        return carry

    lax.fori_loop(0, 3, project, 0)
    weights_copy.wait()
    delta_ref[...] = lax.dot_general(
        gos_ref[...], held_ref[...], NT, preferred_element_type=F32
    ).astype(BF)

    low = iota((WCAP, 128), 1) < 64
    zero = jnp.zeros((), BF)

    def both(value):
        return jnp.concatenate([jnp.where(low, value, zero), jnp.where(low, zero, value)], axis=0)

    def attend(w, carry):
        at = pl.ds(pl.multiple_of(w * WCAP, WCAP), WCAP)
        filled = jnp.broadcast_to(column(win_ref[:, at]) >= 0, (WCAP, WCAP))[None]
        for p in range(6):
            q_at = pl.ds(p * 128, 128)
            k_at = pl.ds(D + p * 128, 128)
            v_at = pl.ds(2 * D + p * 128, 128)
            q = packed_ref[at, q_at]
            k_both = both(packed_ref[at, k_at])
            v_both = both(packed_ref[at, v_at])
            d = delta_ref[at, q_at]
            scaled = q * jnp.asarray(0.125, BF)
            scores = lax.dot_general(k_both, scaled, NT, preferred_element_type=F32)
            scores = jnp.where(filled, scores.reshape(2, WCAP, WCAP), BIG_NEGATIVE)
            expo = jnp.exp(scores - jnp.max(scores, axis=1, keepdims=True))
            probs = expo * (1.0 / jnp.sum(expo, axis=1, keepdims=True))
            weights = probs.astype(BF)
            mixed = lax.dot_general(
                weights.reshape(2 * WCAP, WCAP), v_both, TN, preferred_element_type=F32
            )
            mixed_ref[at, q_at] = mixed.astype(BF)
            dweights = lax.dot_general(v_both, d, NT, preferred_element_type=F32)
            dweights = dweights.reshape(2, WCAP, WCAP)
            inner = jnp.sum(dweights * probs, axis=1, keepdims=True)
            dscaled = (probs * (dweights - inner) * 0.125).astype(BF)
            dq = lax.dot_general(
                dscaled.reshape(2 * WCAP, WCAP), k_both, TN, preferred_element_type=F32
            )
            dpacked_ref[at, q_at] = dq.astype(BF)
            beside = jnp.concatenate([dscaled[0], dscaled[1]], axis=1)
            dpacked_ref[at, k_at] = dot(beside, both(q)).astype(BF)
            beside = jnp.concatenate([weights[0], weights[1]], axis=1)
            dpacked_ref[at, v_at] = dot(beside, both(d)).astype(BF)
        return carry

    lax.fori_loop(0, SLOTS // WCAP, attend, 0, unroll=True)
    dnormed = lax.dot_general(
        dpacked_ref[...], wqkv_ref[...], NT, preferred_element_type=F32
    ).astype(BF)
    dn_ref[...] = dnormed
    unit, _ = normalised(xs_ref[...].astype(F32))
    gain_sum_ref[...] = jnp.sum(dnormed.astype(F32) * unit, axis=0, keepdims=True)


def back_body(
    xs_ref, gos_ref, mixed_ref, dn_ref, win_ref, gain_ref, wout_ref, t_ref, g_ref, kept_ref, cat_ref,
):
    gain = gain_ref[...]
    projected = dot(mixed_ref[...], wout_ref[...])
    cat_ref[:, :D] = (xs_ref[...].astype(F32) + projected).astype(BF)
    for w in range(4):
        at = slice(w * WCAP, (w + 1) * WCAP)
        unit, inv_std = normalised(xs_ref[at, :].astype(F32))
        dnormed = dn_ref[at, :].astype(F32)
        dunit = dnormed * gain
        dcentre = inv_std * (
            dunit
            - jnp.mean(dunit, axis=-1, keepdims=True)
            - unit * jnp.mean(dunit * unit, axis=-1, keepdims=True)
        )
        cat_ref[at, D:] = (gos_ref[at, :].astype(F32) + dcentre).astype(BF)
    back = one_hot(iota((480, SLOTS), 0) == win_ref[...])
    kept_ref[...] = dot(back[:ROWS], cat_ref[...]).astype(BF)
    sent = dot(back[ROWS:], cat_ref[...]).astype(BF).reshape(7, 32, WIDE)
    t_ref[...] = sent[:, :, :D]
    g_ref[...] = sent[:, :, D:]


def join_body(kept_ref, t_refs, g_refs, send_ref, out_ref, grad_ref, own_ref, rows_ref, sems):
    copies = fetches(t_refs, g_refs, DOWN, rows_ref, 0, sems)
    copies.append(pltpu.make_async_copy(kept_ref, own_ref, sems.at[2, 0]))
    for copy in copies:
        copy.start()
    chosen = named(send_ref)
    for copy in copies:
        copy.wait()
    for part, out in enumerate((out_ref, grad_ref)):
        at = slice(part * D, (part + 1) * D)
        back = lax.dot_general(chosen, rows_ref[:, at], TN, preferred_element_type=F32)
        out[...] = (own_ref[:, at].astype(F32) + back).astype(BF)


def sum2_body(me_ref, got_ref, out_ref):
    total = jnp.sum(got_ref[...].astype(F32), axis=0)
    for i in range(4):
        rows = jnp.concatenate([total[4 * i : 4 * (i + 1)], jnp.zeros((4, COLS), F32)])
        out_ref[(me_ref[0] // 2) ^ i] = rows.astype(BF)


def sum3_body(got_ref, qkv_ref, out_ref, gain_ref):
    total = jnp.sum(got_ref[...].astype(F32), axis=0)
    qkv_ref[...] = total[:3, : 3 * D]
    for g in range(3):
        out_ref[g : g + 1, :] = total[3:4, g * D : (g + 1) * D]
    gain_ref[...] = total[:3, 3 * D :]


def call(body, shapes, *args, scratch=(), smem=(), outside=(), mib=SMALL):
    tree = jax.tree.structure(args)
    count = tree.num_leaves

    def flat(*refs):
        body(*jax.tree.unflatten(tree, refs[:count]), *refs[count:])

    return pl.pallas_call(
        flat,
        out_shape=[jax.ShapeDtypeStruct(shape, dtype) for shape, dtype in shapes],
        in_specs=[ANY if i in outside else SMEM if i in smem else VMEM for i in range(count)],
        out_specs=[VMEM] * len(shapes),
        scratch_shapes=list(scratch),
        compiler_params=pltpu.CompilerParams(vmem_limit_bytes=mib * 1024 * 1024),
    )(*jax.tree.leaves(args))


def on_device(tokens, norm_gain, w_qkv, w_out, send_rows, window_rows, grad_out):
    gain = norm_gain.reshape(1, D)
    me = lax.axis_index("gz").astype(jnp.int32).reshape(1)
    me, tokens, grad_out = lax.optimization_barrier((me, tokens, grad_out))
    lists = ((7, 32, D), BF)
    blocks = call(pack_body, [lists, lists], tokens, grad_out, send_rows)
    up = [[blocks[0]], [blocks[1]]]
    places = starts()
    for number in range(3):
        up = step(up, places, UP, number, 1)
    arrived_t, arrived_g = up[0][1:], up[1][1:]

    slot, wide, half = ((SLOTS, D), BF), ((SLOTS, 3 * D), BF), ((HALF, COLS), BF)
    xs, gos, normed, mixed, dpacked, dn, gain_sum = call(
        main_body,
        [slot, slot, slot, slot, wide, slot, ((1, D), F32)],
        tokens, grad_out, arrived_t, arrived_g, window_rows, gain, w_qkv, w_out,
        scratch=[
            pltpu.VMEM((SLOTS, WIDE), BF),
            pltpu.VMEM(*wide),
            pltpu.VMEM(*slot),
            pltpu.VMEM((D, D), BF),
            pltpu.SemaphoreType.DMA((3, 8)),
        ],
        outside=(0, 1, 2, 3, 4, 5, 6, 7, 11),
        mib=MAIN,
    )
    operands = (me, normed, mixed, gos, dpacked, gain_sum)
    (sent,) = call(functools.partial(half_sums, 1), [half], *operands, smem=(0,), mib=SUMS)
    got = crossed(sent, "gz", 1)
    sent, xs = lax.optimization_barrier((sent, xs))
    back_t, back_g, kept = call(
        back_body,
        [lists, lists, ((ROWS, WIDE), BF)],
        xs, gos, mixed, dn, window_rows, gain, w_out,
        scratch=[pltpu.VMEM((SLOTS, WIDE), BF)],
        mib=BACK,
    )
    places = starts()
    down = step([[back_t], [back_g]], places, DOWN, 0, -1)
    (paired,) = call(functools.partial(half_sums, 0), [half], *operands, got, smem=(0,), mib=SUMS)
    paired, down = lax.optimization_barrier((paired, down))
    spread = lax.all_to_all(paired, ("gx", "gy"), split_axis=0, concat_axis=0, tiled=True)
    (part,) = call(sum2_body, [((4, 8, COLS), BF)], me, spread.reshape(32, 16, COLS), smem=(0,))
    part, down = lax.optimization_barrier((part, down))
    down = step(down, places, DOWN, 1, -1)
    down = step(down, places, DOWN, 2, -1)
    groups = [[2 * i + core for i in range(4)] for core in range(2)]
    last = lax.all_to_all(
        part, "gz", split_axis=0, concat_axis=0, tiled=True, axis_index_groups=groups
    )
    grad_qkv, grad_proj, gain_rows = call(
        sum3_body, [((3, 3 * D), F32), ((3, D), F32), ((3, 128), F32)], last
    )

    block_out, grad_tokens = call(
        join_body,
        [((ROWS, D), BF), ((ROWS, D), BF)],
        kept, down[0][1:], down[1][1:], send_rows,
        scratch=[
            pltpu.VMEM((ROWS, WIDE), BF),
            pltpu.VMEM((224, WIDE), BF),
            pltpu.SemaphoreType.DMA((3, 8)),
        ],
        outside=range(7),
    )
    return (block_out, grad_tokens, gain_rows[:, 0], grad_qkv, grad_proj)


def solution(mesh):
    spread = P(AXES, None)
    in_specs = (spread, P(), P(), P(), P(AXES, None, None), spread, spread)
    out_specs = (spread, spread, P(AXES), spread, spread)
    return jax.shard_map(
        on_device, mesh=mesh, in_specs=in_specs, out_specs=out_specs, check_vma=False
    )
```

```python
import functools

import jax
import jax.numpy as jnp
from jax import lax
from jax.experimental import pallas as pl
from jax.experimental.pallas import tpu as pltpu
from jax.sharding import PartitionSpec as P

D = 768
WCAP = 128
SLOTS = 512
ROWS = 256
WIDE = 2 * D
HALF = 512
MAIN, BACK, SUMS, SMALL = 18, 16, 12, 6
COLS = 3 * D + 128
AXES = ("gx", "gy", "gz")
UP = (("gx", "gy", "gz"), ("gz", "gx", "gy"))
DOWN = (("gz", "gy", "gx"), ("gx", "gz", "gy"))
EPSILON = 1e-06
BIG_NEGATIVE = -1e30
BF = jnp.bfloat16
F32 = jnp.float32
NT = (((1,), (1,)), ((), ()))
TN = (((0,), (0,)), ((), ()))
VMEM = pl.BlockSpec(memory_space=pltpu.VMEM)
SMEM = pl.BlockSpec(memory_space=pltpu.SMEM)
ANY = pl.BlockSpec(memory_space=pl.ANY)


def dot(a, b):
    return jnp.dot(a, b, preferred_element_type=F32)


def iota(shape, dim):
    return lax.broadcasted_iota(jnp.int32, shape, dim)


def column(row):
    n = row.shape[1]
    spread = jnp.broadcast_to(row.astype(F32), (n, n))
    return jnp.sum(jnp.where(iota((n, n), 0) == iota((n, n), 1), spread, 0.0), axis=1, keepdims=True)


def one_hot(condition):
    return jnp.where(condition, 1.0, 0.0).astype(BF)


def passed_along(value, axis, steps):
    count = lax.axis_size(axis)
    initial, last = (max(0, -steps), min(count, count - steps))
    return lax.ppermute(value, axis, [(source, source + steps) for source in range(initial, last)])


def bit(k, axis):
    return k // (4, 2, 1)[AXES.index(axis)] % 2


def stage(arrays, place, axis, steps):
    moving = [k for k in range(1, 8) if bit(k, axis)]
    blocks = [lax.slice_in_dim(arrays[place[k][0]], place[k][1], place[k][1] + 1) for k in moving]
    for i, k in enumerate(moving):
        place[k] = (len(arrays), i)
    return [*arrays, passed_along(jnp.concatenate(blocks), axis, steps)]


def starts():
    return [{k: (0, k - 1) for k in range(1, 8)} for _ in range(2)]


def step(pair, places, ways, number, steps):
    return [
        stage(arrays, place, way[number], steps) for arrays, place, way in zip(pair, places, ways)
    ]


def arrival(axes):
    for k in range(1, 8):
        stage = max(s for s, axis in enumerate(axes) if bit(k, axis))
        moving = [m for m in range(1, 8) if bit(m, axes[stage])]
        yield stage, moving.index(k)


def crossed(value, axis, mask):
    count = lax.axis_size(axis)
    return lax.ppermute(value, axis, [(source, source ^ mask) for source in range(count)])


def named(send_ref):
    rows = [one_hot(iota((32, ROWS), 1).astype(F32) == column(send_ref[0, k : k + 1, :])) for k in range(7)]
    return jnp.concatenate(rows, axis=0)


def fetches(t_refs, g_refs, axes, to_ref, start, sems):
    copies = []
    for part, (refs, way) in enumerate(((t_refs, axes[0]), (g_refs, axes[1]))):
        for k, (stage, i) in enumerate(arrival(way)):
            at = to_ref.at[pl.ds(start + 32 * k, 32), pl.ds(part * D, D)]
            copies.append(pltpu.make_async_copy(refs[stage].at[i], at, sems.at[part, k]))
    return copies


def pack_body(tok_ref, go_ref, send_ref, *outs):
    chosen = named(send_ref)
    for part, ref in enumerate((tok_ref, go_ref)):
        outs[part][...] = dot(chosen, ref[...]).astype(BF).reshape(7, 32, D)


def normalised(x):
    centred = x - jnp.mean(x, axis=-1, keepdims=True)
    inv_std = lax.rsqrt(jnp.mean(centred * centred, axis=-1, keepdims=True) + EPSILON)
    return centred * inv_std, inv_std


def first_row(gz, core, block):
    gx, gy, z_hi = block // 16, block % 16 // 4, block % 4
    return ((gx * 4 + gy) * 8 + ((z_hi * 2 + core) ^ gz)) * 3


def half_place(gz, core):
    j = iota((HALF, 1), 0)
    row = jnp.where(j % 4 < 3, first_row(gz, core, j // 4) + j % 4, -1)
    return iota((HALF, D), 1) == row


def with_other(total, at, rest):
    return total + rest[0][:, at].astype(F32) if len(rest) == 2 else total


def half_sums(core, me_ref, normed_ref, mixed_ref, gos_ref, dpacked_ref, gain_ref, *rest):
    out_ref = rest[-1]
    gz = me_ref[0]
    place = half_place(gz, core)
    turned = lax.dot_general(one_hot(place), normed_ref[...], NT, preferred_element_type=F32).astype(BF)
    i = iota((384, 1), 0)
    picks = one_hot(iota((384, D), 1) == first_row(gz, core, i % 128) + i // 128)
    picks = lax.dot_general(picks, mixed_ref[...], NT, preferred_element_type=F32).astype(BF)
    proj = dot(picks, gos_ref[...]).astype(BF)
    j = iota((HALF, 1), 0)
    widen = one_hot(iota((HALF, 128), 1) == jnp.where(j % 4 == 3, j // 4, -1))
    for g in range(3):
        at = slice(g * D, (g + 1) * D)
        total = dot(turned, dpacked_ref[:, at]) + dot(widen, proj[g * 128 : (g + 1) * 128])
        out_ref[:, at] = with_other(total, at, rest).astype(BF)
    gains = jnp.sum(jnp.where(place, gain_ref[...], 0.0), axis=1, keepdims=True)
    gains = jnp.broadcast_to(gains, (HALF, 128))
    at = slice(3 * D, COLS)
    out_ref[:, at] = with_other(gains, at, rest).astype(BF)


def main_body(
    tok_ref, go_ref, t_refs, g_refs, win_ref, gain_ref, wqkv_ref, wout_ref,
    xs_ref, gos_ref, normed_ref, mixed_ref, dpacked_ref, dn_ref, gain_sum_ref,
    rows_ref, packed_ref, delta_ref, held_ref, sems,
):
    copies = fetches(t_refs, g_refs, UP, rows_ref, ROWS, sems)
    own = rows_ref.at[pl.ds(0, ROWS), :]
    copies.append(pltpu.make_async_copy(tok_ref, own.at[:, pl.ds(0, D)], sems.at[0, 7]))
    copies.append(pltpu.make_async_copy(go_ref, own.at[:, pl.ds(D, D)], sems.at[1, 7]))
    weights_copy = pltpu.make_async_copy(wout_ref, held_ref, sems.at[2, 0])
    for copy in copies:
        copy.start()
    weights_copy.start()
    rows_ref[480:, :] = jnp.zeros((32, WIDE), BF)
    gain = gain_ref[...]
    for copy in copies:
        copy.wait()

    def gather_window(w, carry):
        at = pl.ds(pl.multiple_of(w * WCAP, WCAP), WCAP)
        picks = one_hot(iota((WCAP, SLOTS), 1).astype(F32) == column(win_ref[:, at]))
        taken = dot(picks, rows_ref[...])
        x = taken[:, :D]
        xs_ref[at, :] = x.astype(BF)
        gos_ref[at, :] = taken[:, D:].astype(BF)
        unit, _ = normalised(x)
        normed_ref[at, :] = (unit * gain).astype(BF)
        return carry

    lax.fori_loop(0, SLOTS // WCAP, gather_window, 0, unroll=True)

    def project(c, carry):
        at = pl.ds(pl.multiple_of(c * D, D), D)
        packed_ref[:, at] = dot(normed_ref[...], wqkv_ref[:, at]).astype(BF)
        return carry

    lax.fori_loop(0, 3, project, 0)
    weights_copy.wait()
    delta_ref[...] = lax.dot_general(
        gos_ref[...], held_ref[...], NT, preferred_element_type=F32
    ).astype(BF)

    low = iota((WCAP, 128), 1) < 64
    zero = jnp.zeros((), BF)

    def both(value):
        return jnp.concatenate([jnp.where(low, value, zero), jnp.where(low, zero, value)], axis=0)

    def attend(w, carry):
        at = pl.ds(pl.multiple_of(w * WCAP, WCAP), WCAP)
        filled = jnp.broadcast_to(column(win_ref[:, at]) >= 0, (WCAP, WCAP))[None]
        for p in range(6):
            q_at = pl.ds(p * 128, 128)
            k_at = pl.ds(D + p * 128, 128)
            v_at = pl.ds(2 * D + p * 128, 128)
            q = packed_ref[at, q_at]
            k_both = both(packed_ref[at, k_at])
            v_both = both(packed_ref[at, v_at])
            d = delta_ref[at, q_at]
            scaled = q * jnp.asarray(0.125, BF)
            scores = lax.dot_general(k_both, scaled, NT, preferred_element_type=F32)
            scores = jnp.where(filled, scores.reshape(2, WCAP, WCAP), BIG_NEGATIVE)
            expo = jnp.exp(scores - jnp.max(scores, axis=1, keepdims=True))
            probs = expo * (1.0 / jnp.sum(expo, axis=1, keepdims=True))
            weights = probs.astype(BF)
            mixed = lax.dot_general(
                weights.reshape(2 * WCAP, WCAP), v_both, TN, preferred_element_type=F32
            )
            mixed_ref[at, q_at] = mixed.astype(BF)
            dweights = lax.dot_general(v_both, d, NT, preferred_element_type=F32)
            dweights = dweights.reshape(2, WCAP, WCAP)
            inner = jnp.sum(dweights * probs, axis=1, keepdims=True)
            dscaled = (probs * (dweights - inner) * 0.125).astype(BF)
            dq = lax.dot_general(
                dscaled.reshape(2 * WCAP, WCAP), k_both, TN, preferred_element_type=F32
            )
            dpacked_ref[at, q_at] = dq.astype(BF)
            beside = jnp.concatenate([dscaled[0], dscaled[1]], axis=1)
            dpacked_ref[at, k_at] = dot(beside, both(q)).astype(BF)
            beside = jnp.concatenate([weights[0], weights[1]], axis=1)
            dpacked_ref[at, v_at] = dot(beside, both(d)).astype(BF)
        return carry

    lax.fori_loop(0, SLOTS // WCAP, attend, 0, unroll=True)
    dnormed = lax.dot_general(
        dpacked_ref[...], wqkv_ref[...], NT, preferred_element_type=F32
    ).astype(BF)
    dn_ref[...] = dnormed
    unit, _ = normalised(xs_ref[...].astype(F32))
    gain_sum_ref[...] = jnp.sum(dnormed.astype(F32) * unit, axis=0, keepdims=True)


def back_body(
    xs_ref, gos_ref, mixed_ref, dn_ref, win_ref, gain_ref, wout_ref, t_ref, g_ref, kept_ref, cat_ref,
):
    gain = gain_ref[...]
    projected = dot(mixed_ref[...], wout_ref[...])
    cat_ref[:, :D] = (xs_ref[...].astype(F32) + projected).astype(BF)
    for w in range(4):
        at = slice(w * WCAP, (w + 1) * WCAP)
        unit, inv_std = normalised(xs_ref[at, :].astype(F32))
        dnormed = dn_ref[at, :].astype(F32)
        dunit = dnormed * gain
        dcentre = inv_std * (
            dunit
            - jnp.mean(dunit, axis=-1, keepdims=True)
            - unit * jnp.mean(dunit * unit, axis=-1, keepdims=True)
        )
        cat_ref[at, D:] = (gos_ref[at, :].astype(F32) + dcentre).astype(BF)
    back = one_hot(iota((480, SLOTS), 0) == win_ref[...])
    kept_ref[...] = dot(back[:ROWS], cat_ref[...]).astype(BF)
    sent = dot(back[ROWS:], cat_ref[...]).astype(BF).reshape(7, 32, WIDE)
    t_ref[...] = sent[:, :, :D]
    g_ref[...] = sent[:, :, D:]


def join_body(kept_ref, t_refs, g_refs, send_ref, out_ref, grad_ref, own_ref, rows_ref, sems):
    copies = fetches(t_refs, g_refs, DOWN, rows_ref, 0, sems)
    copies.append(pltpu.make_async_copy(kept_ref, own_ref, sems.at[2, 0]))
    for copy in copies:
        copy.start()
    chosen = named(send_ref)
    for copy in copies:
        copy.wait()
    for part, out in enumerate((out_ref, grad_ref)):
        at = slice(part * D, (part + 1) * D)
        back = lax.dot_general(chosen, rows_ref[:, at], TN, preferred_element_type=F32)
        out[...] = (own_ref[:, at].astype(F32) + back).astype(BF)


def sum2_body(me_ref, got_ref, out_ref):
    total = jnp.sum(got_ref[...].astype(F32), axis=0)
    for i in range(4):
        rows = jnp.concatenate([total[4 * i : 4 * (i + 1)], jnp.zeros((4, COLS), F32)])
        out_ref[(me_ref[0] // 2) ^ i] = rows.astype(BF)


def sum3_body(got_ref, qkv_ref, out_ref, gain_ref):
    total = jnp.sum(got_ref[...].astype(F32), axis=0)
    qkv_ref[...] = total[:3, : 3 * D]
    for g in range(3):
        out_ref[g : g + 1, :] = total[3:4, g * D : (g + 1) * D]
    gain_ref[...] = total[:3, 3 * D :]


def call(body, shapes, *args, scratch=(), smem=(), outside=(), mib=SMALL):
    tree = jax.tree.structure(args)
    count = tree.num_leaves

    def flat(*refs):
        body(*jax.tree.unflatten(tree, refs[:count]), *refs[count:])

    return pl.pallas_call(
        flat,
        out_shape=[jax.ShapeDtypeStruct(shape, dtype) for shape, dtype in shapes],
        in_specs=[ANY if i in outside else SMEM if i in smem else VMEM for i in range(count)],
        out_specs=[VMEM] * len(shapes),
        scratch_shapes=list(scratch),
        compiler_params=pltpu.CompilerParams(vmem_limit_bytes=mib * 1024 * 1024),
    )(*jax.tree.leaves(args))


def on_device(tokens, norm_gain, w_qkv, w_out, send_rows, window_rows, grad_out):
    gain = norm_gain.reshape(1, D)
    me = lax.axis_index("gz").astype(jnp.int32).reshape(1)
    me, tokens, grad_out = lax.optimization_barrier((me, tokens, grad_out))
    lists = ((7, 32, D), BF)
    blocks = call(pack_body, [lists, lists], tokens, grad_out, send_rows)
    up = [[blocks[0]], [blocks[1]]]
    places = starts()
    for number in range(3):
        up = step(up, places, UP, number, 1)
    arrived_t, arrived_g = up[0][1:], up[1][1:]

    slot, wide, half = ((SLOTS, D), BF), ((SLOTS, 3 * D), BF), ((HALF, COLS), BF)
    xs, gos, normed, mixed, dpacked, dn, gain_sum = call(
        main_body,
        [slot, slot, slot, slot, wide, slot, ((1, D), F32)],
        tokens, grad_out, arrived_t, arrived_g, window_rows, gain, w_qkv, w_out,
        scratch=[
            pltpu.VMEM((SLOTS, WIDE), BF),
            pltpu.VMEM(*wide),
            pltpu.VMEM(*slot),
            pltpu.VMEM((D, D), BF),
            pltpu.SemaphoreType.DMA((3, 8)),
        ],
        outside=(0, 1, 2, 3, 4, 5, 6, 7, 11),
        mib=MAIN,
    )
    operands = (me, normed, mixed, gos, dpacked, gain_sum)
    (sent,) = call(functools.partial(half_sums, 1), [half], *operands, smem=(0,), mib=SUMS)
    got = crossed(sent, "gz", 1)
    sent, xs = lax.optimization_barrier((sent, xs))
    back_t, back_g, kept = call(
        back_body,
        [lists, lists, ((ROWS, WIDE), BF)],
        xs, gos, mixed, dn, window_rows, gain, w_out,
        scratch=[pltpu.VMEM((SLOTS, WIDE), BF)],
        mib=BACK,
    )
    places = starts()
    down = step([[back_t], [back_g]], places, DOWN, 0, -1)
    (paired,) = call(functools.partial(half_sums, 0), [half], *operands, got, smem=(0,), mib=SUMS)
    spread = lax.all_to_all(paired, ("gx", "gy"), split_axis=0, concat_axis=0, tiled=True)
    (part,) = call(sum2_body, [((4, 8, COLS), BF)], me, spread.reshape(32, 16, COLS), smem=(0,))
    part, down = lax.optimization_barrier((part, down))
    down = step(down, places, DOWN, 1, -1)
    down = step(down, places, DOWN, 2, -1)
    groups = [[2 * i + core for i in range(4)] for core in range(2)]
    last = lax.all_to_all(
        part, "gz", split_axis=0, concat_axis=0, tiled=True, axis_index_groups=groups
    )
    grad_qkv, grad_proj, gain_rows = call(
        sum3_body, [((3, 3 * D), F32), ((3, D), F32), ((3, 128), F32)], last
    )

    block_out, grad_tokens = call(
        join_body,
        [((ROWS, D), BF), ((ROWS, D), BF)],
        kept, down[0][1:], down[1][1:], send_rows,
        scratch=[
            pltpu.VMEM((ROWS, WIDE), BF),
            pltpu.VMEM((224, WIDE), BF),
            pltpu.SemaphoreType.DMA((3, 8)),
        ],
        outside=range(7),
    )
    return (block_out, grad_tokens, gain_rows[:, 0], grad_qkv, grad_proj)


def solution(mesh):
    spread = P(AXES, None)
    in_specs = (spread, P(), P(), P(), P(AXES, None, None), spread, spread)
    out_specs = (spread, spread, P(AXES), spread, spread)
    return jax.shard_map(
        on_device, mesh=mesh, in_specs=in_specs, out_specs=out_specs, check_vma=False
    )
```

```python
import functools

import jax
import jax.numpy as jnp
from jax import lax
from jax.experimental import pallas as pl
from jax.experimental.pallas import tpu as pltpu
from jax.sharding import PartitionSpec as P

D = 768
WCAP = 128
SLOTS = 512
ROWS = 256
WIDE = 2 * D
HALF = 512
MAIN, BACK, SUMS, SMALL = 18, 16, 12, 6
COLS = 3 * D + 128
AXES = ("gx", "gy", "gz")
UP = (("gx", "gy", "gz"), ("gz", "gx", "gy"))
DOWN = (("gz", "gy", "gx"), ("gx", "gz", "gy"))
EPSILON = 1e-06
BIG_NEGATIVE = -1e30
BF = jnp.bfloat16
F32 = jnp.float32
NT = (((1,), (1,)), ((), ()))
TN = (((0,), (0,)), ((), ()))
VMEM = pl.BlockSpec(memory_space=pltpu.VMEM)
SMEM = pl.BlockSpec(memory_space=pltpu.SMEM)
ANY = pl.BlockSpec(memory_space=pl.ANY)


def dot(a, b):
    return jnp.dot(a, b, preferred_element_type=F32)


def iota(shape, dim):
    return lax.broadcasted_iota(jnp.int32, shape, dim)


def column(row):
    n = row.shape[1]
    spread = jnp.broadcast_to(row.astype(F32), (n, n))
    return jnp.sum(jnp.where(iota((n, n), 0) == iota((n, n), 1), spread, 0.0), axis=1, keepdims=True)


def one_hot(condition):
    return jnp.where(condition, 1.0, 0.0).astype(BF)


def passed_along(value, axis, steps):
    count = lax.axis_size(axis)
    initial, last = (max(0, -steps), min(count, count - steps))
    return lax.ppermute(value, axis, [(source, source + steps) for source in range(initial, last)])


def bit(k, axis):
    return k // (4, 2, 1)[AXES.index(axis)] % 2


def stage(arrays, place, axis, steps):
    moving = [k for k in range(1, 8) if bit(k, axis)]
    blocks = [lax.slice_in_dim(arrays[place[k][0]], place[k][1], place[k][1] + 1) for k in moving]
    for i, k in enumerate(moving):
        place[k] = (len(arrays), i)
    return [*arrays, passed_along(jnp.concatenate(blocks), axis, steps)]


def starts():
    return [{k: (0, k - 1) for k in range(1, 8)} for _ in range(2)]


def step(pair, places, ways, number, steps):
    return [
        stage(arrays, place, way[number], steps) for arrays, place, way in zip(pair, places, ways)
    ]


def arrival(axes):
    for k in range(1, 8):
        stage = max(s for s, axis in enumerate(axes) if bit(k, axis))
        moving = [m for m in range(1, 8) if bit(m, axes[stage])]
        yield stage, moving.index(k)


def crossed(value, axis, mask):
    count = lax.axis_size(axis)
    return lax.ppermute(value, axis, [(source, source ^ mask) for source in range(count)])


def named(send_ref):
    rows = [one_hot(iota((32, ROWS), 1).astype(F32) == column(send_ref[0, k : k + 1, :])) for k in range(7)]
    return jnp.concatenate(rows, axis=0)


def fetches(t_refs, g_refs, axes, to_ref, start, sems):
    copies = []
    for part, (refs, way) in enumerate(((t_refs, axes[0]), (g_refs, axes[1]))):
        for k, (stage, i) in enumerate(arrival(way)):
            at = to_ref.at[pl.ds(start + 32 * k, 32), pl.ds(part * D, D)]
            copies.append(pltpu.make_async_copy(refs[stage].at[i], at, sems.at[part, k]))
    return copies


def pack_body(tok_ref, go_ref, send_ref, *outs):
    chosen = named(send_ref)
    for part, ref in enumerate((tok_ref, go_ref)):
        outs[part][...] = dot(chosen, ref[...]).astype(BF).reshape(7, 32, D)


def normalised(x):
    centred = x - jnp.mean(x, axis=-1, keepdims=True)
    inv_std = lax.rsqrt(jnp.mean(centred * centred, axis=-1, keepdims=True) + EPSILON)
    return centred * inv_std, inv_std


def first_row(gz, core, block):
    gx, gy, z_hi = block // 16, block % 16 // 4, block % 4
    return ((gx * 4 + gy) * 8 + ((z_hi * 2 + core) ^ gz)) * 3


def half_place(gz, core):
    j = iota((HALF, 1), 0)
    row = jnp.where(j % 4 < 3, first_row(gz, core, j // 4) + j % 4, -1)
    return iota((HALF, D), 1) == row


def with_other(total, at, rest):
    return total + rest[0][:, at].astype(F32) if len(rest) == 2 else total


def half_sums(core, me_ref, normed_ref, mixed_ref, gos_ref, dpacked_ref, gain_ref, *rest):
    out_ref = rest[-1]
    gz = me_ref[0]
    place = half_place(gz, core)
    turned = lax.dot_general(one_hot(place), normed_ref[...], NT, preferred_element_type=F32).astype(BF)
    i = iota((384, 1), 0)
    picks = one_hot(iota((384, D), 1) == first_row(gz, core, i % 128) + i // 128)
    picks = lax.dot_general(picks, mixed_ref[...], NT, preferred_element_type=F32).astype(BF)
    proj = dot(picks, gos_ref[...]).astype(BF)
    j = iota((HALF, 1), 0)
    widen = one_hot(iota((HALF, 128), 1) == jnp.where(j % 4 == 3, j // 4, -1))
    for g in range(3):
        at = slice(g * D, (g + 1) * D)
        total = dot(turned, dpacked_ref[:, at]) + dot(widen, proj[g * 128 : (g + 1) * 128])
        out_ref[:, at] = with_other(total, at, rest).astype(BF)
    gains = jnp.sum(jnp.where(place, gain_ref[...], 0.0), axis=1, keepdims=True)
    gains = jnp.broadcast_to(gains, (HALF, 128))
    at = slice(3 * D, COLS)
    out_ref[:, at] = with_other(gains, at, rest).astype(BF)


def main_body(
    tok_ref, go_ref, t_refs, g_refs, win_ref, gain_ref, wqkv_ref, wout_ref,
    xs_ref, gos_ref, normed_ref, mixed_ref, dpacked_ref, dn_ref, gain_sum_ref,
    rows_ref, packed_ref, delta_ref, held_ref, sems,
):
    copies = fetches(t_refs, g_refs, UP, rows_ref, ROWS, sems)
    own = rows_ref.at[pl.ds(0, ROWS), :]
    copies.append(pltpu.make_async_copy(tok_ref, own.at[:, pl.ds(0, D)], sems.at[0, 7]))
    copies.append(pltpu.make_async_copy(go_ref, own.at[:, pl.ds(D, D)], sems.at[1, 7]))
    weights_copy = pltpu.make_async_copy(wout_ref, held_ref, sems.at[2, 0])
    for copy in copies:
        copy.start()
    weights_copy.start()
    rows_ref[480:, :] = jnp.zeros((32, WIDE), BF)
    gain = gain_ref[...]
    for copy in copies:
        copy.wait()

    def gather_window(w, carry):
        at = pl.ds(pl.multiple_of(w * WCAP, WCAP), WCAP)
        picks = one_hot(iota((WCAP, SLOTS), 1).astype(F32) == column(win_ref[:, at]))
        taken = dot(picks, rows_ref[...])
        x = taken[:, :D]
        xs_ref[at, :] = x.astype(BF)
        gos_ref[at, :] = taken[:, D:].astype(BF)
        unit, _ = normalised(x)
        normed_ref[at, :] = (unit * gain).astype(BF)
        return carry

    lax.fori_loop(0, SLOTS // WCAP, gather_window, 0, unroll=True)

    def project(c, carry):
        at = pl.ds(pl.multiple_of(c * D, D), D)
        packed_ref[:, at] = dot(normed_ref[...], wqkv_ref[:, at]).astype(BF)
        return carry

    lax.fori_loop(0, 3, project, 0)
    weights_copy.wait()
    delta_ref[...] = lax.dot_general(
        gos_ref[...], held_ref[...], NT, preferred_element_type=F32
    ).astype(BF)

    low = iota((WCAP, 128), 1) < 64
    zero = jnp.zeros((), BF)

    def both(value):
        return jnp.concatenate([jnp.where(low, value, zero), jnp.where(low, zero, value)], axis=0)

    def attend(w, carry):
        at = pl.ds(pl.multiple_of(w * WCAP, WCAP), WCAP)
        filled = jnp.broadcast_to(column(win_ref[:, at]) >= 0, (WCAP, WCAP))[None]
        for p in range(6):
            q_at = pl.ds(p * 128, 128)
            k_at = pl.ds(D + p * 128, 128)
            v_at = pl.ds(2 * D + p * 128, 128)
            q = packed_ref[at, q_at]
            k_both = both(packed_ref[at, k_at])
            v_both = both(packed_ref[at, v_at])
            d = delta_ref[at, q_at]
            scaled = q * jnp.asarray(0.125, BF)
            scores = lax.dot_general(k_both, scaled, NT, preferred_element_type=F32)
            scores = jnp.where(filled, scores.reshape(2, WCAP, WCAP), BIG_NEGATIVE)
            expo = jnp.exp(scores - jnp.max(scores, axis=1, keepdims=True))
            probs = expo * (1.0 / jnp.sum(expo, axis=1, keepdims=True))
            weights = probs.astype(BF)
            mixed = lax.dot_general(
                weights.reshape(2 * WCAP, WCAP), v_both, TN, preferred_element_type=F32
            )
            mixed_ref[at, q_at] = mixed.astype(BF)
            dweights = lax.dot_general(v_both, d, NT, preferred_element_type=F32)
            dweights = dweights.reshape(2, WCAP, WCAP)
            inner = jnp.sum(dweights * probs, axis=1, keepdims=True)
            dscaled = (probs * (dweights - inner) * 0.125).astype(BF)
            dq = lax.dot_general(
                dscaled.reshape(2 * WCAP, WCAP), k_both, TN, preferred_element_type=F32
            )
            dpacked_ref[at, q_at] = dq.astype(BF)
            beside = jnp.concatenate([dscaled[0], dscaled[1]], axis=1)
            dpacked_ref[at, k_at] = dot(beside, both(q)).astype(BF)
            beside = jnp.concatenate([weights[0], weights[1]], axis=1)
            dpacked_ref[at, v_at] = dot(beside, both(d)).astype(BF)
        return carry

    lax.fori_loop(0, SLOTS // WCAP, attend, 0, unroll=True)
    dnormed = lax.dot_general(
        dpacked_ref[...], wqkv_ref[...], NT, preferred_element_type=F32
    ).astype(BF)
    dn_ref[...] = dnormed
    unit, _ = normalised(xs_ref[...].astype(F32))
    gain_sum_ref[...] = jnp.sum(dnormed.astype(F32) * unit, axis=0, keepdims=True)


def back_body(
    xs_ref, gos_ref, mixed_ref, dn_ref, win_ref, gain_ref, wout_ref, t_ref, g_ref, kept_ref, cat_ref,
):
    gain = gain_ref[...]
    projected = dot(mixed_ref[...], wout_ref[...])
    cat_ref[:, :D] = (xs_ref[...].astype(F32) + projected).astype(BF)
    for w in range(4):
        at = slice(w * WCAP, (w + 1) * WCAP)
        unit, inv_std = normalised(xs_ref[at, :].astype(F32))
        dnormed = dn_ref[at, :].astype(F32)
        dunit = dnormed * gain
        dcentre = inv_std * (
            dunit
            - jnp.mean(dunit, axis=-1, keepdims=True)
            - unit * jnp.mean(dunit * unit, axis=-1, keepdims=True)
        )
        cat_ref[at, D:] = (gos_ref[at, :].astype(F32) + dcentre).astype(BF)
    back = one_hot(iota((480, SLOTS), 0) == win_ref[...])
    kept_ref[...] = dot(back[:ROWS], cat_ref[...]).astype(BF)
    sent = dot(back[ROWS:], cat_ref[...]).astype(BF).reshape(7, 32, WIDE)
    t_ref[...] = sent[:, :, :D]
    g_ref[...] = sent[:, :, D:]


def join_body(kept_ref, t_refs, g_refs, send_ref, out_ref, grad_ref, own_ref, rows_ref, sems):
    copies = fetches(t_refs, g_refs, DOWN, rows_ref, 0, sems)
    copies.append(pltpu.make_async_copy(kept_ref, own_ref, sems.at[2, 0]))
    for copy in copies:
        copy.start()
    chosen = named(send_ref)
    for copy in copies:
        copy.wait()
    for part, out in enumerate((out_ref, grad_ref)):
        at = slice(part * D, (part + 1) * D)
        back = lax.dot_general(chosen, rows_ref[:, at], TN, preferred_element_type=F32)
        out[...] = (own_ref[:, at].astype(F32) + back).astype(BF)


def sum2_body(me_ref, got_ref, out_ref):
    total = jnp.sum(got_ref[...].astype(F32), axis=0)
    for i in range(4):
        rows = jnp.concatenate([total[4 * i : 4 * (i + 1)], jnp.zeros((4, COLS), F32)])
        out_ref[(me_ref[0] // 2) ^ i] = rows.astype(BF)


def sum3_body(got_ref, qkv_ref, out_ref, gain_ref):
    total = jnp.sum(got_ref[...].astype(F32), axis=0)
    qkv_ref[...] = total[:3, : 3 * D]
    for g in range(3):
        out_ref[g : g + 1, :] = total[3:4, g * D : (g + 1) * D]
    gain_ref[...] = total[:3, 3 * D :]


def call(body, shapes, *args, scratch=(), smem=(), outside=(), mib=SMALL):
    tree = jax.tree.structure(args)
    count = tree.num_leaves

    def flat(*refs):
        body(*jax.tree.unflatten(tree, refs[:count]), *refs[count:])

    return pl.pallas_call(
        flat,
        out_shape=[jax.ShapeDtypeStruct(shape, dtype) for shape, dtype in shapes],
        in_specs=[ANY if i in outside else SMEM if i in smem else VMEM for i in range(count)],
        out_specs=[VMEM] * len(shapes),
        scratch_shapes=list(scratch),
        compiler_params=pltpu.CompilerParams(vmem_limit_bytes=mib * 1024 * 1024),
    )(*jax.tree.leaves(args))


def on_device(tokens, norm_gain, w_qkv, w_out, send_rows, window_rows, grad_out):
    gain = norm_gain.reshape(1, D)
    me = lax.axis_index("gz").astype(jnp.int32).reshape(1)
    me, tokens, grad_out = lax.optimization_barrier((me, tokens, grad_out))
    lists = ((7, 32, D), BF)
    blocks = call(pack_body, [lists, lists], tokens, grad_out, send_rows)
    up = [[blocks[0]], [blocks[1]]]
    places = starts()
    for number in range(3):
        up = step(up, places, UP, number, 1)
    arrived_t, arrived_g = up[0][1:], up[1][1:]

    slot, wide, half = ((SLOTS, D), BF), ((SLOTS, 3 * D), BF), ((HALF, COLS), BF)
    xs, gos, normed, mixed, dpacked, dn, gain_sum = call(
        main_body,
        [slot, slot, slot, slot, wide, slot, ((1, D), F32)],
        tokens, grad_out, arrived_t, arrived_g, window_rows, gain, w_qkv, w_out,
        scratch=[
            pltpu.VMEM((SLOTS, WIDE), BF),
            pltpu.VMEM(*wide),
            pltpu.VMEM(*slot),
            pltpu.VMEM((D, D), BF),
            pltpu.SemaphoreType.DMA((3, 8)),
        ],
        outside=(0, 1, 2, 3, 4, 5, 6, 7, 11),
        mib=MAIN,
    )
    operands = (me, normed, mixed, gos, dpacked, gain_sum)
    (sent,) = call(functools.partial(half_sums, 1), [half], *operands, smem=(0,), mib=SUMS)
    got = crossed(sent, "gz", 1)
    sent, xs = lax.optimization_barrier((sent, xs))
    back_t, back_g, kept = call(
        back_body,
        [lists, lists, ((ROWS, WIDE), BF)],
        xs, gos, mixed, dn, window_rows, gain, w_out,
        scratch=[pltpu.VMEM((SLOTS, WIDE), BF)],
        mib=BACK,
    )
    places = starts()
    down = step([[back_t], [back_g]], places, DOWN, 0, -1)
    (paired,) = call(functools.partial(half_sums, 0), [half], *operands, got, smem=(0,), mib=SUMS)
    paired, down[0] = lax.optimization_barrier((paired, down[0]))
    spread = lax.all_to_all(paired, ("gx", "gy"), split_axis=0, concat_axis=0, tiled=True)
    (part,) = call(sum2_body, [((4, 8, COLS), BF)], me, spread.reshape(32, 16, COLS), smem=(0,))
    part, down = lax.optimization_barrier((part, down))
    down = step(down, places, DOWN, 1, -1)
    down = step(down, places, DOWN, 2, -1)
    groups = [[2 * i + core for i in range(4)] for core in range(2)]
    last = lax.all_to_all(
        part, "gz", split_axis=0, concat_axis=0, tiled=True, axis_index_groups=groups
    )
    grad_qkv, grad_proj, gain_rows = call(
        sum3_body, [((3, 3 * D), F32), ((3, D), F32), ((3, 128), F32)], last
    )

    block_out, grad_tokens = call(
        join_body,
        [((ROWS, D), BF), ((ROWS, D), BF)],
        kept, down[0][1:], down[1][1:], send_rows,
        scratch=[
            pltpu.VMEM((ROWS, WIDE), BF),
            pltpu.VMEM((224, WIDE), BF),
            pltpu.SemaphoreType.DMA((3, 8)),
        ],
        outside=range(7),
    )
    return (block_out, grad_tokens, gain_rows[:, 0], grad_qkv, grad_proj)


def solution(mesh):
    spread = P(AXES, None)
    in_specs = (spread, P(), P(), P(), P(AXES, None, None), spread, spread)
    out_specs = (spread, spread, P(AXES), spread, spread)
    return jax.shard_map(
        on_device, mesh=mesh, in_specs=in_specs, out_specs=out_specs, check_vma=False
    )
```
